32 devices in a mesh: gx: 8 (over y, x, core), gy: 4 (over z).
Axes of the slice: x: 2, y: 2, z: 4, core: 2. Of those that a mesh axis runs over, the one named last changes fastest.
Arguments:
- populations: float32 [19, 64, 64, 128], P(None, 'gx', 'gy'), may hold values from 0.02 to 0.1
- solid: int32 [64, 64, 128], P('gx', 'gy'), may hold values 0 or 1
- visible: int32 [4, 4, 8], replicated, may hold values 0 or 1
- omega: float32 [1], replicated, may hold values from 1 to 1.6
- iso_levels: float32 [8], replicated, may hold values from -1 to 1
- iso_index: int32 [4, 4], replicated, may hold values from 0 to 7
Outputs:
- new_populations: float32 [19, 64, 64, 128], P(None, 'gx', 'gy')
- q_field: float32 [64, 64, 128], P('gx', 'gy')
- crossings: float32 [3, 64, 64, 128], P(None, 'gx', 'gy')
The draws below stay inside these ranges and needn't reach their ends.
All inputs are finite; a program needn't handle non-finite values. No bound on the sum of `solid` on one device may be relied on, other than what follows from the above.
Results may differ from the reference program's by a relative error of at most 0.000033.
Values sent between devices are 32-bit elements; how exact they have to be, the bound alone decides.
A program may use at most 64 MiB of HBM per device.

```python
import jax
import jax.numpy as jnp

Q = 19
BRICK = 16
LEVELS = 8
NZ = 128
NX = 64
NY = 64


def touch_ends(values, rng, low, top_value):
    index_at = [jax.random.randint(jax.random.fold_in(rng, axis), (), 0, length) for axis, length in enumerate(values.shape)]
    widest = values.shape.index(max(values.shape))
    neighbour = index_at[:widest] + [(index_at[widest] + 1) % values.shape[widest]] + index_at[widest + 1:]
    return values.at[tuple(index_at)].set(low).at[tuple(neighbour)].set(top_value)


def block_levels(stream_key, extent, pieces, smallest, high):
    factor_of, own = 1.0, jax.random.fold_in(stream_key, 6)
    for position, blocks in pieces:
        steps = jnp.exp(jax.random.uniform(jax.random.fold_in(own, position), (blocks,), jnp.float32, smallest / len(pieces), high / len(pieces)))
        factor_of = factor_of * jnp.repeat(steps, extent[position] // blocks).reshape([-1 if axis == position else 1 for axis in range(len(extent))])
    return factor_of


def setup_inputs(seed: int = 0) -> dict:
    key_list = jax.random.split(jax.random.key(seed), 7)
    populations = jnp.clip(0.02 + 0.08 * jax.random.uniform(key_list[0], (Q, NX, NY, NZ), jnp.float32) ** block_levels(key_list[0], (Q, NX, NY, NZ), ((1, 8), (2, 4)), -0.2, 0.2), 0.02, 0.1)
    solid = touch_ends((jax.random.randint(key_list[1], (NX, NY, NZ), 0, 8) < 1).astype(jnp.int32), jax.random.fold_in(key_list[1], 1), 0, 1)
    visible = touch_ends((jax.random.randint(key_list[2], (NX // BRICK, NY // BRICK, NZ // BRICK), 0, 3) < 1).astype(jnp.int32), jax.random.fold_in(key_list[2], 1), 0, 1)
    omega = jnp.clip(jax.random.uniform(key_list[3], (1,), jnp.float32, 1.0, 1.6), 1.0, 1.6)
    iso_levels = jnp.clip(jax.random.uniform(key_list[4], (LEVELS,), jnp.float32, -1.0, 1.0), -1.0, 1.0)
    iso_index = touch_ends(jax.random.randint(key_list[5], (NX // BRICK, NY // BRICK), 0, LEVELS), jax.random.fold_in(key_list[5], 1), 0, LEVELS - 1).astype(jnp.int32)
    return {"populations": populations, "solid": solid, "visible": visible, "omega": omega, "iso_levels": iso_levels, "iso_index": iso_index}


LATTICE = [(0, 0, 0), (1, 0, 0), (-1, 0, 0), (0, 1, 0), (0, -1, 0), (0, 0, 1), (0, 0, -1),
           (1, 1, 0), (-1, -1, 0), (1, -1, 0), (-1, 1, 0), (1, 0, 1), (-1, 0, -1),
           (1, 0, -1), (-1, 0, 1), (0, 1, 1), (0, -1, -1), (0, 1, -1), (0, -1, 1)]
OPPOSITE = [0, 2, 1, 4, 3, 6, 5, 8, 7, 10, 9, 12, 11, 14, 13, 16, 15, 18, 17]
WEIGHTS = [1.0 / 3.0] + [1.0 / 18.0] * 6 + [1.0 / 36.0] * 12


def moments(stacked):
    density = stacked[0]
    for number in range(1, 19):
        density = density + stacked[number]
    velocity = []
    for direction in range(3):
        total = jnp.zeros_like(density)
        for number in range(19):
            component = LATTICE[number][direction]
            if component == 1:
                total = total + stacked[number]
            elif component == -1:
                total = total - stacked[number]
        velocity.append(total / density)
    return density, velocity


def collide(populations, solid, rate):
    density, velocity = moments(populations)
    speed = velocity[0] * velocity[0] + velocity[1] * velocity[1] + velocity[2] * velocity[2]
    collided = []
    for number in range(19):
        projection = jnp.zeros_like(density)
        for direction in range(3):
            component = LATTICE[number][direction]
            if component == 1:
                projection = projection + velocity[direction]
            elif component == -1:
                projection = projection - velocity[direction]
        equilibrium = WEIGHTS[number] * density * (1.0 + 3.0 * projection + 4.5 * projection * projection - 1.5 * speed)
        relaxed = populations[number] - rate * (populations[number] - equilibrium)
        collided.append(jnp.where(solid == 1, populations[OPPOSITE[number]], relaxed))
    return collided


def central(field, axis):
    return (-jnp.roll(field, -2, axis) + 8.0 * jnp.roll(field, -1, axis)
            - 8.0 * jnp.roll(field, 1, axis) + jnp.roll(field, 2, axis)) / 12.0


def crossing(here, there):
    return jnp.maximum(-here * there, 0.0) / (here * here + there * there + 0.25)


def reference(populations, solid, visible, omega, iso_levels, iso_index):
    collided = collide(populations, solid, omega[0])
    read = [jnp.roll(collided[number], LATTICE[number], axis=(0, 1, 2)) for number in range(19)]
    new_populations = jnp.stack(read)
    flow_density, flow = moments(read)
    grads = [[central(flow[first], second) for second in range(3)] for first in range(3)]
    inner = grads[0][0] * grads[0][0] + grads[1][1] * grads[1][1] + grads[2][2] * grads[2][2]
    inner = inner + 2.0 * (grads[0][1] * grads[1][0] + grads[0][2] * grads[2][0] + grads[1][2] * grads[2][1])
    scaled = -50.0 * inner
    choose = iso_index[:, :, None] == jnp.arange(LEVELS, dtype=jnp.int32)[None, None, :]
    brick_levels = jnp.sum(jnp.where(choose, iso_levels[None, None, :], 0.0), axis=2)
    level = jnp.repeat(jnp.repeat(brick_levels, BRICK, axis=0), BRICK, axis=1)[:, :, None]
    here = scaled - level
    cells = jnp.repeat(jnp.repeat(jnp.repeat(visible, BRICK, axis=0), BRICK, axis=1), BRICK, axis=2)
    shown = cells == 1
    weights = [jnp.where(shown, crossing(here, jnp.roll(scaled, -1, axis) - level), 0.0) for axis in range(3)]
    q_field = jnp.where(shown, scaled, 0.0)
    return new_populations, q_field, jnp.stack(weights)
```

```python
import jax
import jax.numpy as jnp
from jax import lax
from jax.experimental import pallas as pl
from jax.experimental.pallas import tpu as pltpu
from jax.sharding import PartitionSpec as P

BRICK = 16
LATTICE = [
    (0, 0, 0),
    (1, 0, 0),
    (-1, 0, 0),
    (0, 1, 0),
    (0, -1, 0),
    (0, 0, 1),
    (0, 0, -1),
    (1, 1, 0),
    (-1, -1, 0),
    (1, -1, 0),
    (-1, 1, 0),
    (1, 0, 1),
    (-1, 0, -1),
    (1, 0, -1),
    (-1, 0, 1),
    (0, 1, 1),
    (0, -1, -1),
    (0, 1, -1),
    (0, -1, 1),
]
OPPOSITE = [0, 2, 1, 4, 3, 6, 5, 8, 7, 10, 9, 12, 11, 14, 13, 16, 15, 18, 17]
DIRECTIONS = [(-1, 0), (1, 0), (0, -1), (0, 1), (-1, -1), (-1, 1), (1, -1), (1, 1)]
MESH = pl.DeviceIdType.MESH
PAD = 8


def needed_halo(width, height):
    cells = set()
    for x in range(width + 1):
        for y in range(height + 1):
            if x == width and y == height:
                continue
            for step in range(-2, 3):
                cells.add((x + step, y))
                cells.add((x, y + step))
    return {(x, y) for x, y in cells if not (0 <= x < width and 0 <= y < height)}


def message_plan(direction, width, height):
    sx, sy = direction
    halo = needed_halo(width, height)
    pops = [
        k
        for k, c in enumerate(LATTICE)
        if (sx == 0 or c[0] == sx) and (sy == 0 or c[1] == sy)
    ]
    layers, cells = [], []
    if sx and not sy:
        layers = [0, 1, 2] if sx < 0 else [width - 2, width - 1]
    if sy and not sx:
        layers = [0, 1, 2] if sy < 0 else [height - 2, height - 1]
    for x in range(-1, width + 1):
        for y in range(-1, height + 1):
            if (x - sx * width, y - sy * height) not in halo:
                continue
            if sx and sy:
                cells.append((x, y))
            elif sx and 0 <= x < width and not 0 <= y < height:
                cells.append((x, y))
            elif sy and 0 <= y < height and not 0 <= x < width:
                cells.append((x, y))
    return pops, layers, cells


def message_rows(direction, width, height):
    pops, layers, cells = message_plan(direction, width, height)
    line = 1 if direction[0] and direction[1] else (height if direction[0] else width)
    rows = len(pops) * line + 4 * len(layers) * line + 4 * len(cells)
    return -(-rows // 8) * 8


def sums(read):
    n11, n12, n13, n14 = read(11), read(12), read(13), read(14)
    n15, n16, n17, n18 = read(15), read(16), read(17), read(18)
    east = (read(1) + n11) + n13
    west = (read(2) + n12) + n14
    north = (read(3) + n15) + n17
    south = (read(4) + n16) + n18
    n5, n6, n7, n8, n9, n10 = read(5), read(6), read(7), read(8), read(9), read(10)
    density = ((read(0) + n5) + n6) + (east + west) + (north + south) + ((n7 + n8) + (n9 + n10))
    momentum_x = (east - west) + ((n7 - n8) + (n9 - n10))
    momentum_y = (north - south) + ((n7 - n8) - (n9 - n10))
    momentum_z = (n5 - n6) + ((n11 - n12) - (n13 - n14)) + ((n15 - n16) - (n17 - n18))
    return density, momentum_x, momentum_y, momentum_z


def kernel_of(sizes, width, height, depth):
    size_x, size_y = sizes
    plans = [message_plan(d, width, height) for d in DIRECTIONS]

    def kernel(pop_hbm, solid_hbm, visible_hbm, omega_hbm, levels_hbm, index_hbm, new_hbm, q_hbm,
               cross_hbm, pop, solid, visible, omega, levels, index, moved, part, total, flow,
               scaled, q_out, cross_out, *rest):
        sends, recvs = rest[:8], rest[8:16]
        in_sem, send_sem, recv_sem, out_sem = rest[16:]
        ix, iy = lax.axis_index("gx"), lax.axis_index("gy")
        copies = [
            pltpu.make_async_copy(src, dst, in_sem.at[i])
            for i, (src, dst) in enumerate(
                [(pop_hbm, pop), (solid_hbm, solid), (omega_hbm, omega), (visible_hbm, visible),
                 (levels_hbm, levels), (index_hbm, index)]
            )
        ]
        for copy in copies:
            copy.start()
        targets = [
            (lax.rem(ix + sx + size_x, size_x), lax.rem(iy + sy + size_y, size_y))
            for sx, sy in DIRECTIONS
        ]
        barrier = pltpu.get_barrier_semaphore()
        for target in targets:
            pl.semaphore_signal(barrier, inc=1, device_id=target, device_id_type=MESH)

        rows = moved.shape[2]
        blank = jnp.zeros((rows, depth), jnp.float32)

        def clear(x, carry):
            for k in range(19):
                moved[k, x] = blank
            return carry

        lax.fori_loop(0, width + 2, clear, 0)
        for x in (0, width + 3, width + 4):
            for c in range(4):
                total[c, x] = blank
        for copy in copies:
            copy.wait()

        rate = omega[0]
        keep = 1.0 - rate

        def collide(x, carry):
            p = [pop[k, x] for k in range(19)]
            wall = solid[x] == 1
            density, mx, my, mz = sums(lambda k: p[k])
            inverse = 1.0 / density
            velocity = (mx * inverse, my * inverse, mz * inverse)
            base = 1.0 - 1.5 * (
                velocity[0] * velocity[0] + velocity[1] * velocity[1] + velocity[2] * velocity[2]
            )
            scale = rate * density
            heavy, light = scale * (1.0 / 18.0), scale * (1.0 / 36.0)

            def put(k, value):
                cx, cy, cz = LATTICE[k]
                value = jnp.where(wall, p[OPPOSITE[k]], value)
                if cz:
                    value = pltpu.roll(value, cz % depth, 1)
                moved[k, x + (1 + cx), PAD + cy : PAD + cy + height, :] = value

            put(0, keep * p[0] + (scale * (1.0 / 3.0)) * base)
            for k in range(1, 19, 2):
                projection = None
                for direction in range(3):
                    component = LATTICE[k][direction]
                    if component:
                        term = velocity[direction]
                        if projection is None:
                            projection = term if component == 1 else -term
                        else:
                            projection = projection + term if component == 1 else projection - term
                weight = heavy if k < 7 else light
                even = base + 4.5 * (projection * projection)
                odd = 3.0 * projection
                put(k, keep * p[k] + weight * (even + odd))
                put(k + 1, keep * p[k + 1] + weight * (even - odd))
            return carry

        lax.fori_loop(0, width, collide, 0)

        def own_part(x, carry):
            for c, value in enumerate(sums(lambda k: moved[k, x])):
                part[c, x] = value
            return carry

        lax.fori_loop(0, width + 2, own_part, 0)

        def pieces(number):
            sx, sy = DIRECTIONS[number]
            pops, layers, cells = plans[number]
            at, found = 0, []
            from_x = {-1: 0, 0: None, 1: width - 1}[sx]
            from_y = {-1: 0, 0: None, 1: height - 1}[sy]
            for k in pops:
                cx, cy, _ = LATTICE[k]
                if sy == 0:
                    y = slice(PAD + cy, PAD + cy + height)
                    here, there = (k, from_x + cx + 1, y), (k, from_x + cx + 1 - sx * width, y)
                    length = height
                elif sx == 0:
                    x = slice(1 + cx, 1 + cx + width)
                    here = (k, x, PAD + from_y + cy)
                    there = (k, x, PAD + from_y + cy - sy * height)
                    length = width
                else:
                    x, y = from_x + cx + 1, PAD + from_y + cy
                    here = (k, x, slice(y, y + 1))
                    there = (k, x - sx * width, slice(y - sy * height, y - sy * height + 1))
                    length = 1
                found.append((True, at, length, here, there))
                at += length
            for layer in layers:
                for c in range(4):
                    if sy == 0:
                        y = slice(PAD, PAD + height)
                        here, there = (c, layer + 1, y), (c, layer + 2 - sx * width, y)
                        length = height
                    else:
                        here = (c, slice(1, 1 + width), PAD + layer)
                        there = (c, slice(2, 2 + width), PAD + layer - sy * height)
                        length = width
                    found.append((False, at, length, here, there))
                    at += length
            for x, y in cells:
                for c in range(4):
                    here = (c, x + 1, slice(PAD + y, PAD + y + 1))
                    to = PAD + y - sy * height
                    found.append((False, at, 1, here, (c, x + 2 - sx * width, slice(to, to + 1))))
                    at += 1
            return found

        pl.semaphore_wait(barrier, 8)
        remote = []
        for number in (4, 5, 6, 7, 2, 3, 0, 1):
            for is_pop, at, length, here, _ in pieces(number):
                source = moved if is_pop else part
                sends[number][at : at + length, :] = source[here]
            copy = pltpu.make_async_remote_copy(
                src_ref=sends[number],
                dst_ref=recvs[number],
                send_sem=send_sem.at[number],
                recv_sem=recv_sem.at[number],
                device_id=targets[number],
                device_id_type=MESH,
            )
            copy.start()
            remote.append((number, copy))

        for number, copy in remote:
            copy.wait_recv()
            for is_pop, at, length, _, there in pieces(number):
                if is_pop:
                    moved[there] = recvs[number][at : at + length, :]

        new_copy = pltpu.make_async_copy(
            moved.at[:, 1 : 1 + width, PAD : PAD + height, :], new_hbm, out_sem.at[0]
        )
        new_copy.start()

        def all_part(x, carry):
            for c, value in enumerate(sums(lambda k: moved[k, x])):
                total[c, x + 1] = value
            return carry

        lax.fori_loop(0, width + 2, all_part, 0)
        for number in range(8):
            for is_pop, at, length, _, there in pieces(number):
                if not is_pop:
                    total[there] = total[there] + recvs[number][at : at + length, :]

        def divide(x, carry):
            inverse = 1.0 / total[0, x]
            for a in range(3):
                flow[a, x, 0:rows, :] = total[a + 1, x] * inverse
            return carry

        lax.fori_loop(0, width + 5, divide, 0)

        tall = height + 8

        def criterion(x, carry):
            grads = []
            for a in range(3):
                def at(dx, dy):
                    return flow[a, x + 2 + dx, PAD + dy : PAD + dy + tall, :]

                centre = at(0, 0)
                along_x = 8.0 * (at(1, 0) - at(-1, 0)) - (at(2, 0) - at(-2, 0))
                along_y = 8.0 * (at(0, 1) - at(0, -1)) - (at(0, 2) - at(0, -2))
                along_z = 8.0 * (
                    pltpu.roll(centre, depth - 1, 1) - pltpu.roll(centre, 1, 1)
                ) - (pltpu.roll(centre, depth - 2, 1) - pltpu.roll(centre, 2, 1))
                grads.append((along_x, along_y, along_z))
            inner = grads[0][0] * grads[0][0] + grads[1][1] * grads[1][1] + grads[2][2] * grads[2][2]
            inner = inner + 2.0 * (
                grads[0][1] * grads[1][0] + grads[0][2] * grads[2][0] + grads[1][2] * grads[2][1]
            )
            scaled[x] = (-50.0 / 144.0) * inner
            return carry

        lax.fori_loop(0, width + 1, criterion, 0)

        brick_x, brick_y = (ix * width) // BRICK, (iy * height) // BRICK
        chosen = index[brick_x, brick_y]
        level = jnp.float32(0.0)
        for number in range(levels.shape[0]):
            level = jnp.where(chosen == number, levels[number], level)
        lane = lax.broadcasted_iota(jnp.int32, (height, depth), 1) // BRICK
        seen = jnp.zeros((height, depth), jnp.int32)
        for number in range(depth // BRICK):
            seen = jnp.where(lane == number, visible[brick_x, brick_y, number], seen)
        shown = seen == 1

        def edges(x, carry):
            inside = scaled[x, 0:height, :]
            here = inside - level
            square = here * here + 0.25
            q_out[x] = jnp.where(shown, inside, 0.0)
            theres = (
                scaled[x + 1, 0:height, :] - level,
                scaled[x, 1 : 1 + height, :] - level,
                pltpu.roll(here, depth - 1, 1),
            )
            for direction, there in enumerate(theres):
                weight = jnp.maximum(-here * there, 0.0) / (square + there * there)
                cross_out[direction, x] = jnp.where(shown, weight, 0.0)
            return carry

        lax.fori_loop(0, width, edges, 0)
        last = [
            pltpu.make_async_copy(q_out, q_hbm, out_sem.at[1]),
            pltpu.make_async_copy(cross_out, cross_hbm, out_sem.at[2]),
        ]
        for copy in last:
            copy.start()
        for _, copy in remote:
            copy.wait_send()
        new_copy.wait()
        for copy in last:
            copy.wait()

    return kernel


def solution(mesh):
    sizes = (mesh.shape["gx"], mesh.shape["gy"])

    def per_device(populations, solid, visible, omega, iso_levels, iso_index):
        _, width, height, depth = populations.shape
        rows = PAD + height + 8
        f32 = jnp.float32
        messages = [
            pltpu.VMEM((message_rows(d, width, height), depth), f32) for d in DIRECTIONS
        ]
        anywhere = pl.BlockSpec(memory_space=pl.ANY)
        return pl.pallas_call(
            kernel_of(sizes, width, height, depth),
            out_shape=(
                jax.ShapeDtypeStruct(populations.shape, f32),
                jax.ShapeDtypeStruct((width, height, depth), f32),
                jax.ShapeDtypeStruct((3, width, height, depth), f32),
            ),
            in_specs=[anywhere] * 6,
            out_specs=(anywhere,) * 3,
            scratch_shapes=[
                pltpu.VMEM(populations.shape, f32),
                pltpu.VMEM(solid.shape, jnp.int32),
                pltpu.SMEM(visible.shape, jnp.int32),
                pltpu.SMEM(omega.shape, f32),
                pltpu.SMEM(iso_levels.shape, f32),
                pltpu.SMEM(iso_index.shape, jnp.int32),
                pltpu.VMEM((19, width + 2, rows, depth), f32),
                pltpu.VMEM((4, width + 2, rows, depth), f32),
                pltpu.VMEM((4, width + 5, rows, depth), f32),
                pltpu.VMEM((3, width + 5, rows + 8, depth), f32),
                pltpu.VMEM((width + 1, height + 8, depth), f32),
                pltpu.VMEM((width, height, depth), f32),
                pltpu.VMEM((3, width, height, depth), f32),
            ]
            + messages
            + messages
            + [
                pltpu.SemaphoreType.DMA((6,)),
                pltpu.SemaphoreType.DMA((8,)),
                pltpu.SemaphoreType.DMA((8,)),
                pltpu.SemaphoreType.DMA((3,)),
            ],
            compiler_params=pltpu.CompilerParams(
                collective_id=0, has_side_effects=True, vmem_limit_bytes=40 * 1024 * 1024
            ),
        )(populations, solid, visible, omega, iso_levels, iso_index)

    in_specs = (P(None, "gx", "gy", None), P("gx", "gy", None), P(), P(), P(), P())
    out_specs = (P(None, "gx", "gy", None), P("gx", "gy", None), P(None, "gx", "gy", None))
    return jax.shard_map(
        per_device, mesh=mesh, in_specs=in_specs, out_specs=out_specs, check_vma=False
    )
```

```python
import jax
import jax.numpy as jnp
from jax import lax
from jax.experimental import pallas as pl
from jax.experimental.pallas import tpu as pltpu
from jax.sharding import PartitionSpec as P

BRICK = 16
LATTICE = [
    (0, 0, 0),
    (1, 0, 0),
    (-1, 0, 0),
    (0, 1, 0),
    (0, -1, 0),
    (0, 0, 1),
    (0, 0, -1),
    (1, 1, 0),
    (-1, -1, 0),
    (1, -1, 0),
    (-1, 1, 0),
    (1, 0, 1),
    (-1, 0, -1),
    (1, 0, -1),
    (-1, 0, 1),
    (0, 1, 1),
    (0, -1, -1),
    (0, 1, -1),
    (0, -1, 1),
]
OPPOSITE = [0, 2, 1, 4, 3, 6, 5, 8, 7, 10, 9, 12, 11, 14, 13, 16, 15, 18, 17]
DIRECTIONS = [(-1, 0), (1, 0), (0, -1), (0, 1), (-1, -1), (-1, 1), (1, -1), (1, 1)]
MESH = pl.DeviceIdType.MESH
PAD = 8


def needed_halo(width, height):
    cells = set()
    for x in range(width + 1):
        for y in range(height + 1):
            if x == width and y == height:
                continue
            for step in range(-2, 3):
                cells.add((x + step, y))
                cells.add((x, y + step))
    return {(x, y) for x, y in cells if not (0 <= x < width and 0 <= y < height)}


def message_plan(direction, width, height):
    sx, sy = direction
    halo = needed_halo(width, height)
    pops = [
        k
        for k, c in enumerate(LATTICE)
        if (sx == 0 or c[0] == sx) and (sy == 0 or c[1] == sy)
    ]
    layers, cells = [], []
    if sx and not sy:
        layers = [0, 1, 2] if sx < 0 else [width - 2, width - 1]
    if sy and not sx:
        layers = [0, 1, 2] if sy < 0 else [height - 2, height - 1]
    for x in range(-1, width + 1):
        for y in range(-1, height + 1):
            if (x - sx * width, y - sy * height) not in halo:
                continue
            if sx and sy:
                cells.append((x, y))
            elif sx and 0 <= x < width and not 0 <= y < height:
                cells.append((x, y))
            elif sy and 0 <= y < height and not 0 <= x < width:
                cells.append((x, y))
    return pops, layers, cells


def message_rows(direction, width, height):
    pops, layers, cells = message_plan(direction, width, height)
    line = 1 if direction[0] and direction[1] else (height if direction[0] else width)
    rows = len(pops) * line + 4 * len(layers) * line + 4 * len(cells)
    return -(-rows // 8) * 8


def sums(read):
    n11, n12, n13, n14 = read(11), read(12), read(13), read(14)
    n15, n16, n17, n18 = read(15), read(16), read(17), read(18)
    east = (read(1) + n11) + n13
    west = (read(2) + n12) + n14
    north = (read(3) + n15) + n17
    south = (read(4) + n16) + n18
    n5, n6, n7, n8, n9, n10 = read(5), read(6), read(7), read(8), read(9), read(10)
    density = ((read(0) + n5) + n6) + (east + west) + (north + south) + ((n7 + n8) + (n9 + n10))
    momentum_x = (east - west) + ((n7 - n8) + (n9 - n10))
    momentum_y = (north - south) + ((n7 - n8) - (n9 - n10))
    momentum_z = (n5 - n6) + ((n11 - n12) - (n13 - n14)) + ((n15 - n16) - (n17 - n18))
    return density, momentum_x, momentum_y, momentum_z


def kernel_of(sizes, width, height, depth):
    size_x, size_y = sizes
    plans = [message_plan(d, width, height) for d in DIRECTIONS]

    def kernel(pop_hbm, solid_hbm, omega_hbm, moved, total, pop, solid, omega, *rest):
        sends, recvs = rest[:8], rest[8:16]
        in_sem, send_sem, recv_sem = rest[16:]
        ix, iy = lax.axis_index("gx"), lax.axis_index("gy")
        copies = [
            pltpu.make_async_copy(src, dst, in_sem.at[i])
            for i, (src, dst) in enumerate(
                [(pop_hbm, pop), (solid_hbm, solid), (omega_hbm, omega)]
            )
        ]
        for copy in copies:
            copy.start()
        targets = [
            (lax.rem(ix + sx + size_x, size_x), lax.rem(iy + sy + size_y, size_y))
            for sx, sy in DIRECTIONS
        ]
        barrier = pltpu.get_barrier_semaphore()
        for target in targets:
            pl.semaphore_signal(barrier, inc=1, device_id=target, device_id_type=MESH)

        rows = moved.shape[2]
        blank = jnp.zeros((rows, depth), jnp.float32)

        def clear(x, carry):
            for k in range(19):
                moved[k, x] = blank
            return carry

        lax.fori_loop(0, width + 2, clear, 0)
        for x in (0, width + 3, width + 4):
            for c in range(4):
                total[c, x] = blank
        for copy in copies:
            copy.wait()

        rate = omega[0]
        keep = 1.0 - rate

        def collide(x, carry):
            p = [pop[k, x] for k in range(19)]
            wall = solid[x] == 1
            density, mx, my, mz = sums(lambda k: p[k])
            inverse = 1.0 / density
            velocity = (mx * inverse, my * inverse, mz * inverse)
            base = 1.0 - 1.5 * (
                velocity[0] * velocity[0] + velocity[1] * velocity[1] + velocity[2] * velocity[2]
            )
            scale = rate * density
            heavy, light = scale * (1.0 / 18.0), scale * (1.0 / 36.0)

            def put(k, value):
                cx, cy, cz = LATTICE[k]
                value = jnp.where(wall, p[OPPOSITE[k]], value)
                if cz:
                    value = pltpu.roll(value, cz % depth, 1)
                moved[k, x + (1 + cx), PAD + cy : PAD + cy + height, :] = value

            put(0, keep * p[0] + (scale * (1.0 / 3.0)) * base)
            for k in range(1, 19, 2):
                projection = None
                for direction in range(3):
                    component = LATTICE[k][direction]
                    if component:
                        term = velocity[direction]
                        if projection is None:
                            projection = term if component == 1 else -term
                        else:
                            projection = projection + term if component == 1 else projection - term
                weight = heavy if k < 7 else light
                even = base + 4.5 * (projection * projection)
                odd = 3.0 * projection
                put(k, keep * p[k] + weight * (even + odd))
                put(k + 1, keep * p[k + 1] + weight * (even - odd))
            return carry

        lax.fori_loop(0, width, collide, 0)

        def own_part(x, carry):
            for c, value in enumerate(sums(lambda k: moved[k, x])):
                total[c, x + 1] = value
            return carry

        lax.fori_loop(0, width + 2, own_part, 0)

        def pieces(number):
            sx, sy = DIRECTIONS[number]
            pops, layers, cells = plans[number]
            at, found = 0, []
            from_x = {-1: 0, 0: None, 1: width - 1}[sx]
            from_y = {-1: 0, 0: None, 1: height - 1}[sy]
            for k in pops:
                cx, cy, _ = LATTICE[k]
                if sy == 0:
                    y = slice(PAD + cy, PAD + cy + height)
                    here, there = (k, from_x + cx + 1, y), (k, from_x + cx + 1 - sx * width, y)
                    length = height
                elif sx == 0:
                    x = slice(1 + cx, 1 + cx + width)
                    here = (k, x, PAD + from_y + cy)
                    there = (k, x, PAD + from_y + cy - sy * height)
                    length = width
                else:
                    x, y = from_x + cx + 1, PAD + from_y + cy
                    here = (k, x, slice(y, y + 1))
                    there = (k, x - sx * width, slice(y - sy * height, y - sy * height + 1))
                    length = 1
                found.append((True, at, length, here, there))
                at += length
            for layer in layers:
                for c in range(4):
                    if sy == 0:
                        y = slice(PAD, PAD + height)
                        here, there = (c, layer + 2, y), (c, layer + 2 - sx * width, y)
                        length = height
                    else:
                        here = (c, slice(2, 2 + width), PAD + layer)
                        there = (c, slice(2, 2 + width), PAD + layer - sy * height)
                        length = width
                    found.append((False, at, length, here, there))
                    at += length
            for x, y in cells:
                for c in range(4):
                    here = (c, x + 2, slice(PAD + y, PAD + y + 1))
                    to = PAD + y - sy * height
                    found.append((False, at, 1, here, (c, x + 2 - sx * width, slice(to, to + 1))))
                    at += 1
            return found

        pl.semaphore_wait(barrier, 8)
        remote = []
        for number in (4, 5, 6, 7, 2, 3, 0, 1):
            for is_pop, at, length, here, _ in pieces(number):
                source = moved if is_pop else total
                sends[number][at : at + length, :] = source[here]
            copy = pltpu.make_async_remote_copy(
                src_ref=sends[number],
                dst_ref=recvs[number],
                send_sem=send_sem.at[number],
                recv_sem=recv_sem.at[number],
                device_id=targets[number],
                device_id_type=MESH,
            )
            copy.start()
            remote.append((number, copy))

        remote = dict(remote)
        for number in (0, 1, 4, 5, 6, 7, 2, 3):
            remote[number].wait_recv()
            groups = {}
            for is_pop, at, length, _, there in pieces(number):
                value = recvs[number][at : at + length, :]
                if not is_pop:
                    total[there] = total[there] + value
                    continue
                moved[there] = value
                k, x, y = there
                x = slice(x.start + 1, x.stop + 1) if isinstance(x, slice) else x + 1
                groups.setdefault(LATTICE[k][:2], []).append((LATTICE[k][2], value, x, y))
            for (cx, cy), members in groups.items():
                _, value, x, y = members[0]
                along_z = None
                for cz, other, _, _ in members[1:]:
                    value = value + other
                if len(members) == 3:
                    up = [other for cz, other, _, _ in members if cz == 1][0]
                    down = [other for cz, other, _, _ in members if cz == -1][0]
                    along_z = up - down
                total[0, x, y] = total[0, x, y] + value
                for c, sign in ((1, cx), (2, cy)):
                    if sign:
                        total[c, x, y] = total[c, x, y] + (value if sign == 1 else -value)
                if along_z is not None:
                    total[3, x, y] = total[3, x, y] + along_z

        for copy in remote.values():
            copy.wait_send()

    return kernel


def finish_of(width, height, depth):
    def kernel(moved, total, visible_hbm, levels_hbm, index_hbm, new_hbm, q_hbm, cross_hbm,
               visible, levels, index, flow, scaled, q_out, cross_out, in_sem, out_sem):
        new_copy = pltpu.make_async_copy(
            moved.at[:, 1 : 1 + width, PAD : PAD + height, :], new_hbm, out_sem.at[0]
        )
        new_copy.start()
        copies = [
            pltpu.make_async_copy(src, dst, in_sem.at[i])
            for i, (src, dst) in enumerate(
                [(visible_hbm, visible), (levels_hbm, levels), (index_hbm, index)]
            )
        ]
        for copy in copies:
            copy.start()
        ix, iy = lax.axis_index("gx"), lax.axis_index("gy")
        rows = total.shape[2]

        def divide(x, carry):
            inverse = 1.0 / total[0, x]
            for a in range(3):
                flow[a, x, 0:rows, :] = total[a + 1, x] * inverse
            return carry

        lax.fori_loop(0, width + 5, divide, 0)

        tall = height + 8

        def criterion(x, carry):
            grads = []
            for a in range(3):
                def at(dx, dy):
                    return flow[a, x + 2 + dx, PAD + dy : PAD + dy + tall, :]

                centre = at(0, 0)
                along_x = 8.0 * (at(1, 0) - at(-1, 0)) - (at(2, 0) - at(-2, 0))
                along_y = 8.0 * (at(0, 1) - at(0, -1)) - (at(0, 2) - at(0, -2))
                along_z = 8.0 * (
                    pltpu.roll(centre, depth - 1, 1) - pltpu.roll(centre, 1, 1)
                ) - (pltpu.roll(centre, depth - 2, 1) - pltpu.roll(centre, 2, 1))
                grads.append((along_x, along_y, along_z))
            inner = grads[0][0] * grads[0][0] + grads[1][1] * grads[1][1] + grads[2][2] * grads[2][2]
            inner = inner + 2.0 * (
                grads[0][1] * grads[1][0] + grads[0][2] * grads[2][0] + grads[1][2] * grads[2][1]
            )
            scaled[x] = (-50.0 / 144.0) * inner
            return carry

        lax.fori_loop(0, width + 1, criterion, 0)

        for copy in copies:
            copy.wait()
        brick_x, brick_y = (ix * width) // BRICK, (iy * height) // BRICK
        chosen = index[brick_x, brick_y]
        level = jnp.float32(0.0)
        for number in range(levels.shape[0]):
            level = jnp.where(chosen == number, levels[number], level)
        lane = lax.broadcasted_iota(jnp.int32, (height, depth), 1) // BRICK
        seen = jnp.zeros((height, depth), jnp.int32)
        for number in range(depth // BRICK):
            seen = jnp.where(lane == number, visible[brick_x, brick_y, number], seen)
        shown = seen == 1

        def edges(x, carry):
            inside = scaled[x, 0:height, :]
            here = inside - level
            square = here * here + 0.25
            q_out[x] = jnp.where(shown, inside, 0.0)
            theres = (
                scaled[x + 1, 0:height, :] - level,
                scaled[x, 1 : 1 + height, :] - level,
                pltpu.roll(here, depth - 1, 1),
            )
            for direction, there in enumerate(theres):
                weight = jnp.maximum(-here * there, 0.0) / (square + there * there)
                cross_out[direction, x] = jnp.where(shown, weight, 0.0)
            return carry

        lax.fori_loop(0, width, edges, 0)
        last = [
            pltpu.make_async_copy(q_out, q_hbm, out_sem.at[1]),
            pltpu.make_async_copy(cross_out, cross_hbm, out_sem.at[2]),
        ]
        for copy in last:
            copy.start()
        new_copy.wait()
        for copy in last:
            copy.wait()

    return kernel


def solution(mesh):
    sizes = (mesh.shape["gx"], mesh.shape["gy"])

    def per_device(populations, solid, visible, omega, iso_levels, iso_index):
        _, width, height, depth = populations.shape
        rows = PAD + height + 8
        f32 = jnp.float32
        messages = [
            pltpu.VMEM((message_rows(d, width, height), depth), f32) for d in DIRECTIONS
        ]
        far = pl.BlockSpec(memory_space=pltpu.HBM)
        near = pl.BlockSpec(memory_space=pltpu.VMEM)
        moved, total = pl.pallas_call(
            kernel_of(sizes, width, height, depth),
            out_shape=(
                jax.ShapeDtypeStruct((19, width + 2, rows, depth), f32),
                jax.ShapeDtypeStruct((4, width + 5, rows, depth), f32),
            ),
            in_specs=[far] * 3,
            out_specs=(near, near),
            scratch_shapes=[
                pltpu.VMEM(populations.shape, f32),
                pltpu.VMEM(solid.shape, jnp.int32),
                pltpu.SMEM(omega.shape, f32),
            ]
            + messages
            + messages
            + [
                pltpu.SemaphoreType.DMA((3,)),
                pltpu.SemaphoreType.DMA((8,)),
                pltpu.SemaphoreType.DMA((8,)),
            ],
            compiler_params=pltpu.CompilerParams(
                collective_id=0, has_side_effects=True, vmem_limit_bytes=24 * 1024 * 1024
            ),
        )(
            pltpu.with_memory_space_constraint(populations, pltpu.HBM),
            pltpu.with_memory_space_constraint(solid, pltpu.HBM),
            omega,
        )
        return pl.pallas_call(
            finish_of(width, height, depth),
            out_shape=(
                jax.ShapeDtypeStruct(populations.shape, f32),
                jax.ShapeDtypeStruct((width, height, depth), f32),
                jax.ShapeDtypeStruct((3, width, height, depth), f32),
            ),
            in_specs=[near, near, far, far, far],
            out_specs=(far, far, far),
            scratch_shapes=[
                pltpu.SMEM(visible.shape, jnp.int32),
                pltpu.SMEM(iso_levels.shape, f32),
                pltpu.SMEM(iso_index.shape, jnp.int32),
                pltpu.VMEM((3, width + 5, rows + 8, depth), f32),
                pltpu.VMEM((width + 1, height + 8, depth), f32),
                pltpu.VMEM((width, height, depth), f32),
                pltpu.VMEM((3, width, height, depth), f32),
                pltpu.SemaphoreType.DMA((3,)),
                pltpu.SemaphoreType.DMA((3,)),
            ],
            compiler_params=pltpu.CompilerParams(vmem_limit_bytes=24 * 1024 * 1024),
        )(moved, total, visible, iso_levels, iso_index)

    in_specs = (P(None, "gx", "gy", None), P("gx", "gy", None), P(), P(), P(), P())
    out_specs = (P(None, "gx", "gy", None), P("gx", "gy", None), P(None, "gx", "gy", None))
    return jax.shard_map(
        per_device, mesh=mesh, in_specs=in_specs, out_specs=out_specs, check_vma=False
    )
```

```python
import jax
import jax.numpy as jnp
from jax import lax
from jax.experimental import pallas as pl
from jax.experimental.pallas import tpu as pltpu
from jax.sharding import PartitionSpec as P

BRICK = 16
LATTICE = [
    (0, 0, 0),
    (1, 0, 0),
    (-1, 0, 0),
    (0, 1, 0),
    (0, -1, 0),
    (0, 0, 1),
    (0, 0, -1),
    (1, 1, 0),
    (-1, -1, 0),
    (1, -1, 0),
    (-1, 1, 0),
    (1, 0, 1),
    (-1, 0, -1),
    (1, 0, -1),
    (-1, 0, 1),
    (0, 1, 1),
    (0, -1, -1),
    (0, 1, -1),
    (0, -1, 1),
]
OPPOSITE = [0, 2, 1, 4, 3, 6, 5, 8, 7, 10, 9, 12, 11, 14, 13, 16, 15, 18, 17]
DIRECTIONS = [(-1, 0), (1, 0), (0, -1), (0, 1), (-1, -1), (-1, 1), (1, -1), (1, 1)]
MESH = pl.DeviceIdType.MESH
CHUNKS = 4
PAD = 8


def needed_halo(width, height):
    cells = set()
    for x in range(width + 1):
        for y in range(height + 1):
            if x == width and y == height:
                continue
            for step in range(-2, 3):
                cells.add((x + step, y))
                cells.add((x, y + step))
    return {(x, y) for x, y in cells if not (0 <= x < width and 0 <= y < height)}


def message_plan(direction, width, height):
    sx, sy = direction
    halo = needed_halo(width, height)
    pops = [
        k
        for k, c in enumerate(LATTICE)
        if (sx == 0 or c[0] == sx) and (sy == 0 or c[1] == sy)
    ]
    layers, cells = [], []
    if sx and not sy:
        layers = [0, 1, 2] if sx < 0 else [width - 2, width - 1]
    if sy and not sx:
        layers = [0, 1, 2] if sy < 0 else [height - 2, height - 1]
    for x in range(-1, width + 1):
        for y in range(-1, height + 1):
            if (x - sx * width, y - sy * height) not in halo:
                continue
            if sx and sy:
                cells.append((x, y))
            elif sx and 0 <= x < width and not 0 <= y < height:
                cells.append((x, y))
            elif sy and 0 <= y < height and not 0 <= x < width:
                cells.append((x, y))
    return pops, layers, cells


UNITS = (
    [(number, True, False) for number in (2, 3, 0, 1)]
    + [(number, True, True) for number in (4, 5, 6, 7)]
    + [(number, False, True) for number in (2, 3, 0, 1)]
)


def message_rows(unit, width, height):
    number, with_pops, with_sums = unit
    direction = DIRECTIONS[number]
    pops, layers, cells = message_plan(direction, width, height)
    pops = pops if with_pops else []
    layers, cells = (layers, cells) if with_sums else ([], [])
    line = 1 if direction[0] and direction[1] else (height if direction[0] else width)
    rows = len(pops) * line + 4 * len(layers) * line + 4 * len(cells)
    return -(-rows // 8) * 8


def sums(read):
    n11, n12, n13, n14 = read(11), read(12), read(13), read(14)
    n15, n16, n17, n18 = read(15), read(16), read(17), read(18)
    east = (read(1) + n11) + n13
    west = (read(2) + n12) + n14
    north = (read(3) + n15) + n17
    south = (read(4) + n16) + n18
    n5, n6, n7, n8, n9, n10 = read(5), read(6), read(7), read(8), read(9), read(10)
    density = ((read(0) + n5) + n6) + (east + west) + (north + south) + ((n7 + n8) + (n9 + n10))
    momentum_x = (east - west) + ((n7 - n8) + (n9 - n10))
    momentum_y = (north - south) + ((n7 - n8) - (n9 - n10))
    momentum_z = (n5 - n6) + ((n11 - n12) - (n13 - n14)) + ((n15 - n16) - (n17 - n18))
    return density, momentum_x, momentum_y, momentum_z


def kernel_of(sizes, width, height, depth):
    size_x, size_y = sizes
    plans = [message_plan(d, width, height) for d in DIRECTIONS]

    def kernel(pop_hbm, solid_hbm, omega_hbm, moved, total, pop, solid, omega, *rest):
        count = len(UNITS)
        sends, recvs = rest[:count], rest[count : 2 * count]
        in_sem, send_sem, recv_sem = rest[2 * count :]
        ix, iy = lax.axis_index("gx"), lax.axis_index("gy")
        layers = width // CHUNKS
        copies = [
            pltpu.make_async_copy(src, dst, in_sem.at[i])
            for i, (src, dst) in enumerate(
                [(solid_hbm, solid), (omega_hbm, omega)]
                + [
                    (pop_hbm.at[:, pl.ds(c * layers, layers)], pop.at[:, pl.ds(c * layers, layers)])
                    for c in range(CHUNKS)
                ]
            )
        ]
        for copy in copies:
            copy.start()
        targets = [
            (lax.rem(ix + sx + size_x, size_x), lax.rem(iy + sy + size_y, size_y))
            for sx, sy in DIRECTIONS
        ]
        barrier = pltpu.get_barrier_semaphore()
        for target in targets:
            pl.semaphore_signal(barrier, inc=1, device_id=target, device_id_type=MESH)

        rows = moved.shape[2]
        blank = jnp.zeros((rows, depth), jnp.float32)

        def clear(x, carry):
            for k in range(19):
                moved[k, x] = blank
            return carry

        lax.fori_loop(0, width + 2, clear, 0)
        for x in (0, width + 3, width + 4):
            for c in range(4):
                total[c, x] = blank
        for copy in copies[:2]:
            copy.wait()

        rate = omega[0]
        keep = 1.0 - rate

        def collide(x, carry):
            p = [pop[k, x] for k in range(19)]
            wall = solid[x] == 1
            density, mx, my, mz = sums(lambda k: p[k])
            inverse = 1.0 / density
            velocity = (mx * inverse, my * inverse, mz * inverse)
            base = 1.0 - 1.5 * (
                velocity[0] * velocity[0] + velocity[1] * velocity[1] + velocity[2] * velocity[2]
            )
            scale = rate * density
            heavy, light = scale * (1.0 / 18.0), scale * (1.0 / 36.0)

            def put(k, value):
                cx, cy, cz = LATTICE[k]
                value = jnp.where(wall, p[OPPOSITE[k]], value)
                if cz:
                    value = pltpu.roll(value, cz % depth, 1)
                moved[k, x + (1 + cx), PAD + cy : PAD + cy + height, :] = value

            put(0, keep * p[0] + (scale * (1.0 / 3.0)) * base)
            for k in range(1, 19, 2):
                projection = None
                for direction in range(3):
                    component = LATTICE[k][direction]
                    if component:
                        term = velocity[direction]
                        if projection is None:
                            projection = term if component == 1 else -term
                        else:
                            projection = projection + term if component == 1 else projection - term
                weight = heavy if k < 7 else light
                even = base + 4.5 * (projection * projection)
                odd = 3.0 * projection
                put(k, keep * p[k] + weight * (even + odd))
                put(k + 1, keep * p[k + 1] + weight * (even - odd))
            return carry

        for c in range(CHUNKS):
            copies[2 + c].wait()
            for x in range(c * layers, (c + 1) * layers):
                collide(x, 0)

        def pieces(unit):
            number, with_pops, with_sums = UNITS[unit]
            sx, sy = DIRECTIONS[number]
            pops, layers, cells = plans[number]
            pops = pops if with_pops else []
            layers, cells = (layers, cells) if with_sums else ([], [])
            at, found = 0, []
            from_x = {-1: 0, 0: None, 1: width - 1}[sx]
            from_y = {-1: 0, 0: None, 1: height - 1}[sy]
            for k in pops:
                cx, cy, _ = LATTICE[k]
                if sy == 0:
                    y = slice(PAD + cy, PAD + cy + height)
                    here, there = (k, from_x + cx + 1, y), (k, from_x + cx + 1 - sx * width, y)
                    length = height
                elif sx == 0:
                    x = slice(1 + cx, 1 + cx + width)
                    here = (k, x, PAD + from_y + cy)
                    there = (k, x, PAD + from_y + cy - sy * height)
                    length = width
                else:
                    x, y = from_x + cx + 1, PAD + from_y + cy
                    here = (k, x, slice(y, y + 1))
                    there = (k, x - sx * width, slice(y - sy * height, y - sy * height + 1))
                    length = 1
                found.append((True, at, length, here, there))
                at += length
            for layer in layers:
                for c in range(4):
                    if sy == 0:
                        y = slice(PAD, PAD + height)
                        here, there = (c, layer + 2, y), (c, layer + 2 - sx * width, y)
                        length = height
                    else:
                        here = (c, slice(2, 2 + width), PAD + layer)
                        there = (c, slice(2, 2 + width), PAD + layer - sy * height)
                        length = width
                    found.append((False, at, length, here, there))
                    at += length
            for x, y in cells:
                for c in range(4):
                    here = (c, x + 2, slice(PAD + y, PAD + y + 1))
                    to = PAD + y - sy * height
                    found.append((False, at, 1, here, (c, x + 2 - sx * width, slice(to, to + 1))))
                    at += 1
            return found

        remote = {}

        def send(unit):
            for is_pop, at, length, here, _ in pieces(unit):
                source = moved if is_pop else total
                sends[unit][at : at + length, :] = source[here]
            copy = pltpu.make_async_remote_copy(
                src_ref=sends[unit],
                dst_ref=recvs[unit],
                send_sem=send_sem.at[unit],
                recv_sem=recv_sem.at[unit],
                device_id=targets[UNITS[unit][0]],
                device_id_type=MESH,
            )
            copy.start()
            remote[unit] = copy

        pl.semaphore_wait(barrier, 8)
        for unit in range(4):
            send(unit)

        def own_part(x, carry):
            for c, value in enumerate(sums(lambda k: moved[k, x, 4 : rows - 4, :])):
                total[c, x + 1, 4 : rows - 4, :] = value
            return carry

        lax.fori_loop(0, width + 2, own_part, 0, unroll=2)

        for unit in range(4, count):
            send(unit)

        for unit in (2, 3, 0, 1, 4, 5, 6, 7, 10, 11, 8, 9):
            remote[unit].wait_recv()
            groups = {}
            for is_pop, at, length, _, there in pieces(unit):
                value = recvs[unit][at : at + length, :]
                if not is_pop:
                    total[there] = total[there] + value
                    continue
                moved[there] = value
                k, x, y = there
                x = slice(x.start + 1, x.stop + 1) if isinstance(x, slice) else x + 1
                groups.setdefault(LATTICE[k][:2], []).append((LATTICE[k][2], value, x, y))
            for (cx, cy), members in groups.items():
                _, value, x, y = members[0]
                along_z = None
                for cz, other, _, _ in members[1:]:
                    value = value + other
                if len(members) == 3:
                    up = [other for cz, other, _, _ in members if cz == 1][0]
                    down = [other for cz, other, _, _ in members if cz == -1][0]
                    along_z = up - down
                total[0, x, y] = total[0, x, y] + value
                for c, sign in ((1, cx), (2, cy)):
                    if sign:
                        total[c, x, y] = total[c, x, y] + (value if sign == 1 else -value)
                if along_z is not None:
                    total[3, x, y] = total[3, x, y] + along_z

        for copy in remote.values():
            copy.wait_send()

    return kernel


def finish_of(width, height, depth):
    def kernel(moved, total, visible_hbm, levels_hbm, index_hbm, new_hbm, q_hbm, cross_hbm,
               visible, levels, index, flow, scaled, q_out, cross_out, in_sem, out_sem):
        new_copy = pltpu.make_async_copy(
            moved.at[:, 1 : 1 + width, PAD : PAD + height, :], new_hbm, out_sem.at[0]
        )
        new_copy.start()
        copies = [
            pltpu.make_async_copy(src, dst, in_sem.at[i])
            for i, (src, dst) in enumerate(
                [(visible_hbm, visible), (levels_hbm, levels), (index_hbm, index)]
            )
        ]
        for copy in copies:
            copy.start()
        ix, iy = lax.axis_index("gx"), lax.axis_index("gy")
        rows = total.shape[2]

        def divide(x, carry):
            inverse = 1.0 / total[0, x, 4 : rows - 4, :]
            for a in range(3):
                flow[a, x, 4 : rows - 4, :] = total[a + 1, x, 4 : rows - 4, :] * inverse
            return carry

        for x in range(width + 5):
            divide(x, 0)

        tall = height + 8

        def criterion(x, carry):
            grads = []
            for a in range(3):
                def at(dx, dy):
                    return flow[a, x + 2 + dx, PAD + dy : PAD + dy + tall, :]

                centre = at(0, 0)
                along_x = 8.0 * (at(1, 0) - at(-1, 0)) - (at(2, 0) - at(-2, 0))
                along_y = 8.0 * (at(0, 1) - at(0, -1)) - (at(0, 2) - at(0, -2))
                along_z = 8.0 * (
                    pltpu.roll(centre, depth - 1, 1) - pltpu.roll(centre, 1, 1)
                ) - (pltpu.roll(centre, depth - 2, 1) - pltpu.roll(centre, 2, 1))
                grads.append((along_x, along_y, along_z))
            inner = grads[0][0] * grads[0][0] + grads[1][1] * grads[1][1] + grads[2][2] * grads[2][2]
            inner = inner + 2.0 * (
                grads[0][1] * grads[1][0] + grads[0][2] * grads[2][0] + grads[1][2] * grads[2][1]
            )
            scaled[x] = (-50.0 / 144.0) * inner
            return carry

        for x in range(width + 1):
            criterion(x, 0)

        for copy in copies:
            copy.wait()
        brick_x, brick_y = (ix * width) // BRICK, (iy * height) // BRICK
        chosen = index[brick_x, brick_y]
        level = jnp.float32(0.0)
        for number in range(levels.shape[0]):
            level = jnp.where(chosen == number, levels[number], level)
        lane = lax.broadcasted_iota(jnp.int32, (height, depth), 1) // BRICK
        seen = jnp.zeros((height, depth), jnp.int32)
        for number in range(depth // BRICK):
            seen = jnp.where(lane == number, visible[brick_x, brick_y, number], seen)
        shown = seen == 1

        def edges(x, carry):
            inside = scaled[x, 0:height, :]
            here = inside - level
            square = here * here + 0.25
            q_out[x] = jnp.where(shown, inside, 0.0)
            theres = (
                scaled[x + 1, 0:height, :] - level,
                scaled[x, 1 : 1 + height, :] - level,
                pltpu.roll(here, depth - 1, 1),
            )
            for direction, there in enumerate(theres):
                weight = jnp.maximum(-here * there, 0.0) / (square + there * there)
                cross_out[direction, x] = jnp.where(shown, weight, 0.0)
            return carry

        for x in range(width):
            edges(x, 0)
        last = [
            pltpu.make_async_copy(q_out, q_hbm, out_sem.at[1]),
            pltpu.make_async_copy(cross_out, cross_hbm, out_sem.at[2]),
        ]
        for copy in last:
            copy.start()
        new_copy.wait()
        for copy in last:
            copy.wait()

    return kernel


def solution(mesh):
    sizes = (mesh.shape["gx"], mesh.shape["gy"])

    def per_device(populations, solid, visible, omega, iso_levels, iso_index):
        _, width, height, depth = populations.shape
        rows = PAD + height + 8
        f32 = jnp.float32
        messages = [
            pltpu.VMEM((message_rows(unit, width, height), depth), f32) for unit in UNITS
        ]
        far = pl.BlockSpec(memory_space=pltpu.HBM)
        near = pl.BlockSpec(memory_space=pltpu.VMEM)
        moved, total = pl.pallas_call(
            kernel_of(sizes, width, height, depth),
            out_shape=(
                jax.ShapeDtypeStruct((19, width + 2, rows, depth), f32),
                jax.ShapeDtypeStruct((4, width + 5, rows, depth), f32),
            ),
            in_specs=[far] * 3,
            out_specs=(near, near),
            scratch_shapes=[
                pltpu.VMEM(populations.shape, f32),
                pltpu.VMEM(solid.shape, jnp.int32),
                pltpu.SMEM(omega.shape, f32),
            ]
            + messages
            + messages
            + [
                pltpu.SemaphoreType.DMA((2 + CHUNKS,)),
                pltpu.SemaphoreType.DMA((len(UNITS),)),
                pltpu.SemaphoreType.DMA((len(UNITS),)),
            ],
            compiler_params=pltpu.CompilerParams(
                collective_id=0, has_side_effects=True, vmem_limit_bytes=24 * 1024 * 1024
            ),
        )(
            pltpu.with_memory_space_constraint(populations, pltpu.HBM),
            pltpu.with_memory_space_constraint(solid, pltpu.HBM),
            omega,
        )
        return pl.pallas_call(
            finish_of(width, height, depth),
            out_shape=(
                jax.ShapeDtypeStruct(populations.shape, f32),
                jax.ShapeDtypeStruct((width, height, depth), f32),
                jax.ShapeDtypeStruct((3, width, height, depth), f32),
            ),
            in_specs=[near, near, far, far, far],
            out_specs=(far, far, far),
            scratch_shapes=[
                pltpu.SMEM(visible.shape, jnp.int32),
                pltpu.SMEM(iso_levels.shape, f32),
                pltpu.SMEM(iso_index.shape, jnp.int32),
                pltpu.VMEM((3, width + 5, rows + 8, depth), f32),
                pltpu.VMEM((width + 1, height + 8, depth), f32),
                pltpu.VMEM((width, height, depth), f32),
                pltpu.VMEM((3, width, height, depth), f32),
                pltpu.SemaphoreType.DMA((3,)),
                pltpu.SemaphoreType.DMA((3,)),
            ],
            compiler_params=pltpu.CompilerParams(vmem_limit_bytes=24 * 1024 * 1024),
        )(moved, total, visible, iso_levels, iso_index)

    in_specs = (P(None, "gx", "gy", None), P("gx", "gy", None), P(), P(), P(), P())
    out_specs = (P(None, "gx", "gy", None), P("gx", "gy", None), P(None, "gx", "gy", None))
    return jax.shard_map(
        per_device, mesh=mesh, in_specs=in_specs, out_specs=out_specs, check_vma=False
    )
```

```python
import jax
import jax.numpy as jnp
from jax import lax
from jax.experimental import pallas as pl
from jax.experimental.pallas import tpu as pltpu
from jax.sharding import PartitionSpec as P

BRICK = 16
LATTICE = [
    (0, 0, 0),
    (1, 0, 0),
    (-1, 0, 0),
    (0, 1, 0),
    (0, -1, 0),
    (0, 0, 1),
    (0, 0, -1),
    (1, 1, 0),
    (-1, -1, 0),
    (1, -1, 0),
    (-1, 1, 0),
    (1, 0, 1),
    (-1, 0, -1),
    (1, 0, -1),
    (-1, 0, 1),
    (0, 1, 1),
    (0, -1, -1),
    (0, 1, -1),
    (0, -1, 1),
]
OPPOSITE = [0, 2, 1, 4, 3, 6, 5, 8, 7, 10, 9, 12, 11, 14, 13, 16, 15, 18, 17]
DIRECTIONS = [(-1, 0), (1, 0), (0, -1), (0, 1), (-1, -1), (-1, 1), (1, -1), (1, 1)]
MESH = pl.DeviceIdType.MESH
CHUNKS = 4
PAD = 8


def needed_halo(width, height):
    cells = set()
    for x in range(width + 1):
        for y in range(height + 1):
            if x == width and y == height:
                continue
            for step in range(-2, 3):
                cells.add((x + step, y))
                cells.add((x, y + step))
    return {(x, y) for x, y in cells if not (0 <= x < width and 0 <= y < height)}


def message_plan(direction, width, height):
    sx, sy = direction
    halo = needed_halo(width, height)
    pops = [
        k
        for k, c in enumerate(LATTICE)
        if (sx == 0 or c[0] == sx) and (sy == 0 or c[1] == sy)
    ]
    layers, cells = [], []
    if sx and not sy:
        layers = [0, 1, 2] if sx < 0 else [width - 2, width - 1]
    if sy and not sx:
        layers = [0, 1, 2] if sy < 0 else [height - 2, height - 1]
    for x in range(-1, width + 1):
        for y in range(-1, height + 1):
            if (x - sx * width, y - sy * height) not in halo:
                continue
            if sx and sy:
                cells.append((x, y))
            elif sx and 0 <= x < width and not 0 <= y < height:
                cells.append((x, y))
            elif sy and 0 <= y < height and not 0 <= x < width:
                cells.append((x, y))
    return pops, layers, cells


def touches(direction, layer, width, height):
    sx, sy = direction
    return layer == (0 if sx + sy < 0 else (width if sx else height) - 1)


UNITS = (
    [(number, True, False) for number in (2, 3, 0, 1)]
    + [(number, True, True) for number in (4, 5, 6, 7)]
    + [(number, False, True) for number in (2, 3, 0, 1)]
)


def message_rows(unit, width, height):
    number, with_pops, with_sums = unit
    direction = DIRECTIONS[number]
    pops, layers, cells = message_plan(direction, width, height)
    pops = pops if with_pops else []
    layers, cells = (layers, cells) if with_sums else ([], [])
    line = 1 if direction[0] and direction[1] else (height if direction[0] else width)
    rows = len(pops) * line + 4 * len(cells)
    for layer in layers:
        rows += 4 * line if touches(direction, layer, width, height) else 3 * line + 2
    for x, y in cells:
        rows -= 0 if 0 <= x < width and 0 <= y < height else 1
    return -(-rows // 8) * 8


def sums(read):
    n11, n12, n13, n14 = read(11), read(12), read(13), read(14)
    n15, n16, n17, n18 = read(15), read(16), read(17), read(18)
    east = (read(1) + n11) + n13
    west = (read(2) + n12) + n14
    north = (read(3) + n15) + n17
    south = (read(4) + n16) + n18
    n5, n6, n7, n8, n9, n10 = read(5), read(6), read(7), read(8), read(9), read(10)
    density = ((read(0) + n5) + n6) + (east + west) + (north + south) + ((n7 + n8) + (n9 + n10))
    momentum_x = (east - west) + ((n7 - n8) + (n9 - n10))
    momentum_y = (north - south) + ((n7 - n8) - (n9 - n10))
    momentum_z = (n5 - n6) + ((n11 - n12) - (n13 - n14)) + ((n15 - n16) - (n17 - n18))
    return density, momentum_x, momentum_y, momentum_z


def kernel_of(sizes, width, height, depth):
    size_x, size_y = sizes
    plans = [message_plan(d, width, height) for d in DIRECTIONS]

    def kernel(pop_hbm, solid_hbm, omega_hbm, moved, total, pop, solid, omega, *rest):
        count = len(UNITS)
        sends, recvs = rest[:count], rest[count : 2 * count]
        in_sem, send_sem, recv_sem = rest[2 * count :]
        ix, iy = lax.axis_index("gx"), lax.axis_index("gy")
        layers = width // CHUNKS
        copies = [
            pltpu.make_async_copy(src, dst, in_sem.at[i])
            for i, (src, dst) in enumerate(
                [(solid_hbm, solid), (omega_hbm, omega)]
                + [
                    (pop_hbm.at[:, pl.ds(c * layers, layers)], pop.at[:, pl.ds(c * layers, layers)])
                    for c in range(CHUNKS)
                ]
            )
        ]
        for copy in copies:
            copy.start()
        targets = [
            (lax.rem(ix + sx + size_x, size_x), lax.rem(iy + sy + size_y, size_y))
            for sx, sy in DIRECTIONS
        ]
        barrier = pltpu.get_barrier_semaphore()
        for target in targets:
            pl.semaphore_signal(barrier, inc=1, device_id=target, device_id_type=MESH)

        rows = moved.shape[2]
        blank = jnp.zeros((rows, depth), jnp.float32)

        def clear(x, carry):
            for k in range(19):
                moved[k, x] = blank
            return carry

        lax.fori_loop(0, width + 2, clear, 0)
        for x in (0, width + 3, width + 4):
            for c in range(4):
                total[c, x] = blank
        for copy in copies[:2]:
            copy.wait()

        rate = omega[0]
        keep = 1.0 - rate

        def collide(x, carry):
            p = [pop[k, x] for k in range(19)]
            wall = solid[x] == 1
            density, mx, my, mz = sums(lambda k: p[k])
            inverse = 1.0 / density
            velocity = (mx * inverse, my * inverse, mz * inverse)
            base = 1.0 - 1.5 * (
                velocity[0] * velocity[0] + velocity[1] * velocity[1] + velocity[2] * velocity[2]
            )
            scale = rate * density
            heavy, light = scale * (1.0 / 18.0), scale * (1.0 / 36.0)

            def put(k, value):
                cx, cy, cz = LATTICE[k]
                value = jnp.where(wall, p[OPPOSITE[k]], value)
                if cz:
                    value = pltpu.roll(value, cz % depth, 1)
                moved[k, x + (1 + cx), PAD + cy : PAD + cy + height, :] = value

            put(0, keep * p[0] + (scale * (1.0 / 3.0)) * base)
            for k in range(1, 19, 2):
                projection = None
                for direction in range(3):
                    component = LATTICE[k][direction]
                    if component:
                        term = velocity[direction]
                        if projection is None:
                            projection = term if component == 1 else -term
                        else:
                            projection = projection + term if component == 1 else projection - term
                weight = heavy if k < 7 else light
                even = base + 4.5 * (projection * projection)
                odd = 3.0 * projection
                put(k, keep * p[k] + weight * (even + odd))
                put(k + 1, keep * p[k + 1] + weight * (even - odd))
            return carry

        for c in range(CHUNKS):
            copies[2 + c].wait()
            for x in range(c * layers, (c + 1) * layers):
                collide(x, 0)

        def pieces(unit):
            number, with_pops, with_sums = UNITS[unit]
            sx, sy = DIRECTIONS[number]
            pops, layers, cells = plans[number]
            pops = pops if with_pops else []
            layers, cells = (layers, cells) if with_sums else ([], [])
            at, found = 0, []
            from_x = {-1: 0, 0: None, 1: width - 1}[sx]
            from_y = {-1: 0, 0: None, 1: height - 1}[sy]
            for k in pops:
                cx, cy, _ = LATTICE[k]
                if sy == 0:
                    y = slice(PAD + cy, PAD + cy + height)
                    here, there = (k, from_x + cx + 1, y), (k, from_x + cx + 1 - sx * width, y)
                    length = height
                elif sx == 0:
                    x = slice(1 + cx, 1 + cx + width)
                    here = (k, x, PAD + from_y + cy)
                    there = (k, x, PAD + from_y + cy - sy * height)
                    length = width
                else:
                    x, y = from_x + cx + 1, PAD + from_y + cy
                    here = (k, x, slice(y, y + 1))
                    there = (k, x - sx * width, slice(y - sy * height, y - sy * height + 1))
                    length = 1
                found.append(("pop", at, length, here, there))
                at += length
            for layer in layers:
                whole = touches(DIRECTIONS[number], layer, width, height)
                for c in range(0 if whole else 1, 4):
                    if sy == 0:
                        y = slice(PAD, PAD + height)
                        here, there = (c, layer + 2, y), (c, layer + 2 - sx * width, y)
                        length = height
                    else:
                        here = (c, slice(2, 2 + width), PAD + layer)
                        there = (c, slice(2, 2 + width), PAD + layer - sy * height)
                        length = width
                    found.append(("sum" if whole else "flow", at, length, here, there))
                    at += length
                for edge in () if whole else (0, (height if sy == 0 else width) - 1):
                    x, y = (layer, edge) if sy == 0 else (edge, layer)
                    row = slice(PAD + y, PAD + y + 1)
                    to = PAD + y - sy * height
                    there = (0, x + 2 - sx * width, slice(to, to + 1))
                    found.append(("sum", at, 1, (0, x + 2, row), there))
                    at += 1
            for x, y in cells:
                for c in range(4):
                    if (c == 1 and not 0 <= x < width) or (c == 2 and not 0 <= y < height):
                        continue
                    here = (c, x + 2, slice(PAD + y, PAD + y + 1))
                    to = PAD + y - sy * height
                    there = (c, x + 2 - sx * width, slice(to, to + 1))
                    kind = "sum"
                    if c == 0 and not 0 <= x < width:
                        kind = ("also", 1, x < 0)
                    if c == 0 and not 0 <= y < height:
                        kind = ("also", 2, y < 0)
                    found.append((kind, at, 1, here, there))
                    at += 1
            return found

        remote = {}

        def inner(length):
            place = lax.broadcasted_iota(jnp.int32, (length, depth), 0)
            return jnp.logical_and(place > 0, place < length - 1)

        def send(unit):
            inverses = {}
            for kind, at, length, here, _ in pieces(unit):
                value = moved[here] if kind == "pop" else total[here]
                if kind == "flow":
                    key = str(here[1:])
                    if key not in inverses:
                        density = total[(0,) + here[1:]]
                        inverses[key] = jnp.where(inner(length), 1.0 / density, 1.0)
                    value = value * inverses[key]
                sends[unit][at : at + length, :] = value
            copy = pltpu.make_async_remote_copy(
                src_ref=sends[unit],
                dst_ref=recvs[unit],
                send_sem=send_sem.at[unit],
                recv_sem=recv_sem.at[unit],
                device_id=targets[UNITS[unit][0]],
                device_id_type=MESH,
            )
            copy.start()
            remote[unit] = copy

        pl.semaphore_wait(barrier, 8)
        for unit in range(4):
            send(unit)

        def own_part(x, carry):
            for c, value in enumerate(sums(lambda k: moved[k, x, 4 : rows - 4, :])):
                total[c, x + 1, 4 : rows - 4, :] = value
            return carry

        lax.fori_loop(0, width + 2, own_part, 0, unroll=2)

        for unit in range(4, count):
            send(unit)

        for unit in (2, 3, 0, 1, 4, 5, 6, 7, 10, 11, 8, 9):
            remote[unit].wait_recv()
            groups = {}
            for kind, at, length, _, there in pieces(unit):
                value = recvs[unit][at : at + length, :]
                if kind != "pop":
                    total[there] = total[there] + value
                    if kind == "flow" and there[0] == 1:
                        density = (0,) + there[1:]
                        total[density] = total[density] + jnp.where(inner(length), 1.0, 0.0)
                    if kind[0] == "also":
                        c = (kind[1],) + there[1:]
                        total[c] = total[c] + (-value if kind[2] else value)
                    continue
                moved[there] = value
                k, x, y = there
                x = slice(x.start + 1, x.stop + 1) if isinstance(x, slice) else x + 1
                groups.setdefault(LATTICE[k][:2], []).append((LATTICE[k][2], value, x, y))
            for (cx, cy), members in groups.items():
                _, value, x, y = members[0]
                along_z = None
                for cz, other, _, _ in members[1:]:
                    value = value + other
                if len(members) == 3:
                    up = [other for cz, other, _, _ in members if cz == 1][0]
                    down = [other for cz, other, _, _ in members if cz == -1][0]
                    along_z = up - down
                total[0, x, y] = total[0, x, y] + value
                for c, sign in ((1, cx), (2, cy)):
                    if sign:
                        total[c, x, y] = total[c, x, y] + (value if sign == 1 else -value)
                if along_z is not None:
                    total[3, x, y] = total[3, x, y] + along_z

        for copy in remote.values():
            copy.wait_send()

    return kernel


def finish_of(width, height, depth):
    def kernel(moved, total, visible_hbm, levels_hbm, index_hbm, new_hbm, q_hbm, cross_hbm,
               visible, levels, index, flow, scaled, q_out, cross_out, in_sem, out_sem):
        new_copy = pltpu.make_async_copy(
            moved.at[:, 1 : 1 + width, PAD : PAD + height, :], new_hbm, out_sem.at[0]
        )
        new_copy.start()
        copies = [
            pltpu.make_async_copy(src, dst, in_sem.at[i])
            for i, (src, dst) in enumerate(
                [(visible_hbm, visible), (levels_hbm, levels), (index_hbm, index)]
            )
        ]
        for copy in copies:
            copy.start()
        ix, iy = lax.axis_index("gx"), lax.axis_index("gy")
        rows = total.shape[2]

        def divide(x, carry):
            inverse = 1.0 / total[0, x, 4 : rows - 4, :]
            for a in range(3):
                flow[a, x, 4 : rows - 4, :] = total[a + 1, x, 4 : rows - 4, :] * inverse
            return carry

        for x in range(width + 5):
            divide(x, 0)

        tall = height + 8

        def criterion(x, carry):
            grads = []
            for a in range(3):
                def at(dx, dy):
                    return flow[a, x + 2 + dx, PAD + dy : PAD + dy + tall, :]

                centre = at(0, 0)
                along_x = 8.0 * (at(1, 0) - at(-1, 0)) - (at(2, 0) - at(-2, 0))
                along_y = 8.0 * (at(0, 1) - at(0, -1)) - (at(0, 2) - at(0, -2))
                along_z = 8.0 * (
                    pltpu.roll(centre, depth - 1, 1) - pltpu.roll(centre, 1, 1)
                ) - (pltpu.roll(centre, depth - 2, 1) - pltpu.roll(centre, 2, 1))
                grads.append((along_x, along_y, along_z))
            inner = grads[0][0] * grads[0][0] + grads[1][1] * grads[1][1] + grads[2][2] * grads[2][2]
            inner = inner + 2.0 * (
                grads[0][1] * grads[1][0] + grads[0][2] * grads[2][0] + grads[1][2] * grads[2][1]
            )
            scaled[x] = (-50.0 / 144.0) * inner
            return carry

        for x in range(width + 1):
            criterion(x, 0)

        for copy in copies:
            copy.wait()
        brick_x, brick_y = (ix * width) // BRICK, (iy * height) // BRICK
        chosen = index[brick_x, brick_y]
        level = jnp.float32(0.0)
        for number in range(levels.shape[0]):
            level = jnp.where(chosen == number, levels[number], level)
        lane = lax.broadcasted_iota(jnp.int32, (height, depth), 1) // BRICK
        seen = jnp.zeros((height, depth), jnp.int32)
        for number in range(depth // BRICK):
            seen = jnp.where(lane == number, visible[brick_x, brick_y, number], seen)
        shown = seen == 1

        def edges(x, carry):
            inside = scaled[x, 0:height, :]
            here = inside - level
            square = here * here + 0.25
            q_out[x] = jnp.where(shown, inside, 0.0)
            theres = (
                scaled[x + 1, 0:height, :] - level,
                scaled[x, 1 : 1 + height, :] - level,
                pltpu.roll(here, depth - 1, 1),
            )
            for direction, there in enumerate(theres):
                weight = jnp.maximum(-here * there, 0.0) / (square + there * there)
                cross_out[direction, x] = jnp.where(shown, weight, 0.0)
            return carry

        for x in range(width):
            edges(x, 0)
        last = [
            pltpu.make_async_copy(q_out, q_hbm, out_sem.at[1]),
            pltpu.make_async_copy(cross_out, cross_hbm, out_sem.at[2]),
        ]
        for copy in last:
            copy.start()
        new_copy.wait()
        for copy in last:
            copy.wait()

    return kernel


def solution(mesh):
    sizes = (mesh.shape["gx"], mesh.shape["gy"])

    def per_device(populations, solid, visible, omega, iso_levels, iso_index):
        _, width, height, depth = populations.shape
        rows = PAD + height + 8
        f32 = jnp.float32
        messages = [
            pltpu.VMEM((message_rows(unit, width, height), depth), f32) for unit in UNITS
        ]
        far = pl.BlockSpec(memory_space=pltpu.HBM)
        near = pl.BlockSpec(memory_space=pltpu.VMEM)
        moved, total = pl.pallas_call(
            kernel_of(sizes, width, height, depth),
            out_shape=(
                jax.ShapeDtypeStruct((19, width + 2, rows, depth), f32),
                jax.ShapeDtypeStruct((4, width + 5, rows, depth), f32),
            ),
            in_specs=[far] * 3,
            out_specs=(near, near),
            scratch_shapes=[
                pltpu.VMEM(populations.shape, f32),
                pltpu.VMEM(solid.shape, jnp.int32),
                pltpu.SMEM(omega.shape, f32),
            ]
            + messages
            + messages
            + [
                pltpu.SemaphoreType.DMA((2 + CHUNKS,)),
                pltpu.SemaphoreType.DMA((len(UNITS),)),
                pltpu.SemaphoreType.DMA((len(UNITS),)),
            ],
            compiler_params=pltpu.CompilerParams(
                collective_id=0, has_side_effects=True, vmem_limit_bytes=24 * 1024 * 1024
            ),
        )(
            pltpu.with_memory_space_constraint(populations, pltpu.HBM),
            pltpu.with_memory_space_constraint(solid, pltpu.HBM),
            omega,
        )
        return pl.pallas_call(
            finish_of(width, height, depth),
            out_shape=(
                jax.ShapeDtypeStruct(populations.shape, f32),
                jax.ShapeDtypeStruct((width, height, depth), f32),
                jax.ShapeDtypeStruct((3, width, height, depth), f32),
            ),
            in_specs=[near, near, far, far, far],
            out_specs=(far, far, far),
            scratch_shapes=[
                pltpu.SMEM(visible.shape, jnp.int32),
                pltpu.SMEM(iso_levels.shape, f32),
                pltpu.SMEM(iso_index.shape, jnp.int32),
                pltpu.VMEM((3, width + 5, rows + 8, depth), f32),
                pltpu.VMEM((width + 1, height + 8, depth), f32),
                pltpu.VMEM((width, height, depth), f32),
                pltpu.VMEM((3, width, height, depth), f32),
                pltpu.SemaphoreType.DMA((3,)),
                pltpu.SemaphoreType.DMA((3,)),
            ],
            compiler_params=pltpu.CompilerParams(vmem_limit_bytes=24 * 1024 * 1024),
        )(moved, total, visible, iso_levels, iso_index)

    in_specs = (P(None, "gx", "gy", None), P("gx", "gy", None), P(), P(), P(), P())
    out_specs = (P(None, "gx", "gy", None), P("gx", "gy", None), P(None, "gx", "gy", None))
    return jax.shard_map(
        per_device, mesh=mesh, in_specs=in_specs, out_specs=out_specs, check_vma=False
    )
```

```python
import jax
import jax.numpy as jnp
from jax import lax
from jax.experimental import pallas as pl
from jax.experimental.pallas import tpu as pltpu
from jax.sharding import PartitionSpec as P

BRICK = 16
LATTICE = [
    (0, 0, 0),
    (1, 0, 0),
    (-1, 0, 0),
    (0, 1, 0),
    (0, -1, 0),
    (0, 0, 1),
    (0, 0, -1),
    (1, 1, 0),
    (-1, -1, 0),
    (1, -1, 0),
    (-1, 1, 0),
    (1, 0, 1),
    (-1, 0, -1),
    (1, 0, -1),
    (-1, 0, 1),
    (0, 1, 1),
    (0, -1, -1),
    (0, 1, -1),
    (0, -1, 1),
]
OPPOSITE = [0, 2, 1, 4, 3, 6, 5, 8, 7, 10, 9, 12, 11, 14, 13, 16, 15, 18, 17]
DIRECTIONS = [(-1, 0), (1, 0), (0, -1), (0, 1), (-1, -1), (-1, 1), (1, -1), (1, 1)]
MESH = pl.DeviceIdType.MESH
CHUNKS = 4
PAD = 8


def needed_halo(width, height):
    cells = set()
    for x in range(width + 1):
        for y in range(height + 1):
            if x == width and y == height:
                continue
            for step in range(-2, 3):
                cells.add((x + step, y))
                cells.add((x, y + step))
    return {(x, y) for x, y in cells if not (0 <= x < width and 0 <= y < height)}


def message_plan(direction, width, height):
    sx, sy = direction
    halo = needed_halo(width, height)
    pops = [
        k
        for k, c in enumerate(LATTICE)
        if (sx == 0 or c[0] == sx) and (sy == 0 or c[1] == sy)
    ]
    layers, cells = [], []
    if sx and not sy:
        layers = [0, 1, 2] if sx < 0 else [width - 2, width - 1]
    if sy and not sx:
        layers = [0, 1, 2] if sy < 0 else [height - 2, height - 1]
    for x in range(-1, width + 1):
        for y in range(-1, height + 1):
            if (x - sx * width, y - sy * height) not in halo:
                continue
            if sx and sy:
                cells.append((x, y))
            elif sx and 0 <= x < width and not 0 <= y < height:
                cells.append((x, y))
            elif sy and 0 <= y < height and not 0 <= x < width:
                cells.append((x, y))
    return pops, layers, cells


def touches(direction, layer, width, height):
    sx, sy = direction
    return layer == (0 if sx + sy < 0 else (width if sx else height) - 1)


UNITS = (
    [(number, True, False) for number in (2, 3, 0, 1)]
    + [(number, True, True) for number in (4, 5, 6, 7)]
    + [(number, False, True) for number in (2, 3, 0, 1)]
)


def message_rows(unit, width, height):
    number, with_pops, with_sums = unit
    direction = DIRECTIONS[number]
    pops, layers, cells = message_plan(direction, width, height)
    pops = pops if with_pops else []
    layers, cells = (layers, cells) if with_sums else ([], [])
    line = 1 if direction[0] and direction[1] else (height if direction[0] else width)
    rows = len(pops) * line + 4 * len(cells)
    for layer in layers:
        rows += 4 * line if touches(direction, layer, width, height) else 3 * line + 2
    for x, y in cells:
        rows -= 0 if 0 <= x < width and 0 <= y < height else 1
    return -(-rows // 8) * 8


def sums(read):
    n11, n12, n13, n14 = read(11), read(12), read(13), read(14)
    n15, n16, n17, n18 = read(15), read(16), read(17), read(18)
    east = (read(1) + n11) + n13
    west = (read(2) + n12) + n14
    north = (read(3) + n15) + n17
    south = (read(4) + n16) + n18
    n5, n6, n7, n8, n9, n10 = read(5), read(6), read(7), read(8), read(9), read(10)
    density = ((read(0) + n5) + n6) + (east + west) + (north + south) + ((n7 + n8) + (n9 + n10))
    momentum_x = (east - west) + ((n7 - n8) + (n9 - n10))
    momentum_y = (north - south) + ((n7 - n8) - (n9 - n10))
    momentum_z = (n5 - n6) + ((n11 - n12) - (n13 - n14)) + ((n15 - n16) - (n17 - n18))
    return density, momentum_x, momentum_y, momentum_z


def kernel_of(sizes, width, height, depth):
    size_x, size_y = sizes
    plans = [message_plan(d, width, height) for d in DIRECTIONS]

    def kernel(pop_hbm, solid_hbm, omega_rows, moved, total, pop, solid, *rest):
        count = len(UNITS)
        sends, recvs = rest[:count], rest[count : 2 * count]
        in_sem, send_sem, recv_sem = rest[2 * count :]
        ix, iy = lax.axis_index("gx"), lax.axis_index("gy")
        layers = width // CHUNKS
        copies = [
            pltpu.make_async_copy(src, dst, in_sem.at[i])
            for i, (src, dst) in enumerate(
                [(solid_hbm, solid)]
                + [
                    (pop_hbm.at[:, pl.ds(c * layers, layers)], pop.at[:, pl.ds(c * layers, layers)])
                    for c in range(CHUNKS)
                ]
            )
        ]
        targets = [
            (lax.rem(ix + sx + size_x, size_x), lax.rem(iy + sy + size_y, size_y))
            for sx, sy in DIRECTIONS
        ]
        barrier = pltpu.get_barrier_semaphore()
        for target in targets:
            pl.semaphore_signal(barrier, inc=1, device_id=target, device_id_type=MESH)
        for copy in copies:
            copy.start()

        rows = moved.shape[2]
        blank = jnp.zeros((rows, depth), jnp.float32)

        def clear(x, carry):
            for k in range(19):
                moved[k, x] = blank
            return carry

        lax.fori_loop(0, width + 2, clear, 0)
        for x in (0, width + 3, width + 4):
            for c in range(4):
                total[c, x] = blank
        for copy in copies[:1]:
            copy.wait()

        rate = omega_rows[0:1, :]
        keep = 1.0 - rate

        def collide(x, carry):
            p = [pop[k, x] for k in range(19)]
            wall = solid[x] == 1
            density, mx, my, mz = sums(lambda k: p[k])
            inverse = 1.0 / density
            velocity = (mx * inverse, my * inverse, mz * inverse)
            base = 1.0 - 1.5 * (
                velocity[0] * velocity[0] + velocity[1] * velocity[1] + velocity[2] * velocity[2]
            )
            scale = rate * density
            heavy, light = scale * (1.0 / 18.0), scale * (1.0 / 36.0)

            def put(k, value):
                cx, cy, cz = LATTICE[k]
                value = jnp.where(wall, p[OPPOSITE[k]], value)
                if cz:
                    value = pltpu.roll(value, cz % depth, 1)
                moved[k, x + (1 + cx), PAD + cy : PAD + cy + height, :] = value

            put(0, keep * p[0] + (scale * (1.0 / 3.0)) * base)
            for k in range(1, 19, 2):
                projection = None
                for direction in range(3):
                    component = LATTICE[k][direction]
                    if component:
                        term = velocity[direction]
                        if projection is None:
                            projection = term if component == 1 else -term
                        else:
                            projection = projection + term if component == 1 else projection - term
                weight = heavy if k < 7 else light
                even = base + 4.5 * (projection * projection)
                odd = 3.0 * projection
                put(k, keep * p[k] + weight * (even + odd))
                put(k + 1, keep * p[k + 1] + weight * (even - odd))
            return carry

        for c in range(CHUNKS):
            copies[1 + c].wait()
            for x in range(c * layers, (c + 1) * layers):
                collide(x, 0)

        def pieces(unit):
            number, with_pops, with_sums = UNITS[unit]
            sx, sy = DIRECTIONS[number]
            pops, layers, cells = plans[number]
            pops = pops if with_pops else []
            layers, cells = (layers, cells) if with_sums else ([], [])
            at, found = 0, []
            from_x = {-1: 0, 0: None, 1: width - 1}[sx]
            from_y = {-1: 0, 0: None, 1: height - 1}[sy]
            for k in pops:
                cx, cy, _ = LATTICE[k]
                if sy == 0:
                    y = slice(PAD + cy, PAD + cy + height)
                    here, there = (k, from_x + cx + 1, y), (k, from_x + cx + 1 - sx * width, y)
                    length = height
                elif sx == 0:
                    x = slice(1 + cx, 1 + cx + width)
                    here = (k, x, PAD + from_y + cy)
                    there = (k, x, PAD + from_y + cy - sy * height)
                    length = width
                else:
                    x, y = from_x + cx + 1, PAD + from_y + cy
                    here = (k, x, slice(y, y + 1))
                    there = (k, x - sx * width, slice(y - sy * height, y - sy * height + 1))
                    length = 1
                found.append(("pop", at, length, here, there))
                at += length
            for layer in layers:
                whole = touches(DIRECTIONS[number], layer, width, height)
                for c in range(0 if whole else 1, 4):
                    if sy == 0:
                        y = slice(PAD, PAD + height)
                        here, there = (c, layer + 2, y), (c, layer + 2 - sx * width, y)
                        length = height
                    else:
                        here = (c, slice(2, 2 + width), PAD + layer)
                        there = (c, slice(2, 2 + width), PAD + layer - sy * height)
                        length = width
                    found.append(("sum" if whole else "flow", at, length, here, there))
                    at += length
                for edge in () if whole else (0, (height if sy == 0 else width) - 1):
                    x, y = (layer, edge) if sy == 0 else (edge, layer)
                    row = slice(PAD + y, PAD + y + 1)
                    to = PAD + y - sy * height
                    there = (0, x + 2 - sx * width, slice(to, to + 1))
                    found.append(("sum", at, 1, (0, x + 2, row), there))
                    at += 1
            for x, y in cells:
                for c in range(4):
                    if (c == 1 and not 0 <= x < width) or (c == 2 and not 0 <= y < height):
                        continue
                    here = (c, x + 2, slice(PAD + y, PAD + y + 1))
                    to = PAD + y - sy * height
                    there = (c, x + 2 - sx * width, slice(to, to + 1))
                    kind = "sum"
                    if c == 0 and not 0 <= x < width:
                        kind = ("also", 1, x < 0)
                    if c == 0 and not 0 <= y < height:
                        kind = ("also", 2, y < 0)
                    found.append((kind, at, 1, here, there))
                    at += 1
            return found

        remote = {}

        def inner(length):
            place = lax.broadcasted_iota(jnp.int32, (length, depth), 0)
            return jnp.logical_and(place > 0, place < length - 1)

        def send(unit):
            inverses = {}
            for kind, at, length, here, _ in pieces(unit):
                value = moved[here] if kind == "pop" else total[here]
                if kind == "flow":
                    key = str(here[1:])
                    if key not in inverses:
                        density = total[(0,) + here[1:]]
                        inverses[key] = jnp.where(inner(length), 1.0 / density, 1.0)
                    value = value * inverses[key]
                sends[unit][at : at + length, :] = value
            copy = pltpu.make_async_remote_copy(
                src_ref=sends[unit],
                dst_ref=recvs[unit],
                send_sem=send_sem.at[unit],
                recv_sem=recv_sem.at[unit],
                device_id=targets[UNITS[unit][0]],
                device_id_type=MESH,
            )
            copy.start()
            remote[unit] = copy

        pl.semaphore_wait(barrier, 8)
        for unit in range(4):
            send(unit)

        def own_part(x, carry):
            for c, value in enumerate(sums(lambda k: moved[k, x, 4 : rows - 4, :])):
                total[c, x + 1, 4 : rows - 4, :] = value
            return carry

        lax.fori_loop(0, width + 2, own_part, 0, unroll=2)

        for unit in range(4, count):
            send(unit)

        for unit in (2, 3, 0, 1, 4, 5, 6, 7, 10, 11, 8, 9):
            remote[unit].wait_recv()
            groups = {}
            for kind, at, length, _, there in pieces(unit):
                value = recvs[unit][at : at + length, :]
                if kind != "pop":
                    total[there] = total[there] + value
                    if kind == "flow" and there[0] == 1:
                        density = (0,) + there[1:]
                        total[density] = total[density] + jnp.where(inner(length), 1.0, 0.0)
                    if kind[0] == "also":
                        c = (kind[1],) + there[1:]
                        total[c] = total[c] + (-value if kind[2] else value)
                    continue
                moved[there] = value
                k, x, y = there
                x = slice(x.start + 1, x.stop + 1) if isinstance(x, slice) else x + 1
                groups.setdefault(LATTICE[k][:2], []).append((LATTICE[k][2], value, x, y))
            for (cx, cy), members in groups.items():
                _, value, x, y = members[0]
                along_z = None
                for cz, other, _, _ in members[1:]:
                    value = value + other
                if len(members) == 3:
                    up = [other for cz, other, _, _ in members if cz == 1][0]
                    down = [other for cz, other, _, _ in members if cz == -1][0]
                    along_z = up - down
                total[0, x, y] = total[0, x, y] + value
                for c, sign in ((1, cx), (2, cy)):
                    if sign:
                        total[c, x, y] = total[c, x, y] + (value if sign == 1 else -value)
                if along_z is not None:
                    total[3, x, y] = total[3, x, y] + along_z

        for copy in remote.values():
            copy.wait_send()

    return kernel


def finish_of(width, height, depth):
    def kernel(moved, total, visible_hbm, levels_hbm, index_hbm, new_hbm, q_hbm, cross_hbm,
               visible, levels, index, flow, scaled, q_out, cross_out, in_sem, out_sem):
        new_copy = pltpu.make_async_copy(
            moved.at[:, 1 : 1 + width, PAD : PAD + height, :], new_hbm, out_sem.at[0]
        )
        new_copy.start()
        copies = [
            pltpu.make_async_copy(src, dst, in_sem.at[i])
            for i, (src, dst) in enumerate(
                [(visible_hbm, visible), (levels_hbm, levels), (index_hbm, index)]
            )
        ]
        for copy in copies:
            copy.start()
        ix, iy = lax.axis_index("gx"), lax.axis_index("gy")
        rows = total.shape[2]

        def divide(x, carry):
            inverse = 1.0 / total[0, x, 4 : rows - 4, :]
            for a in range(3):
                flow[a, x, 4 : rows - 4, :] = total[a + 1, x, 4 : rows - 4, :] * inverse
            return carry

        for x in range(width + 5):
            divide(x, 0)

        tall = height + 8

        def criterion(x, carry):
            grads = []
            for a in range(3):
                def at(dx, dy):
                    return flow[a, x + 2 + dx, PAD + dy : PAD + dy + tall, :]

                centre = at(0, 0)
                along_x = 8.0 * (at(1, 0) - at(-1, 0)) - (at(2, 0) - at(-2, 0))
                along_y = 8.0 * (at(0, 1) - at(0, -1)) - (at(0, 2) - at(0, -2))
                along_z = 8.0 * (
                    pltpu.roll(centre, depth - 1, 1) - pltpu.roll(centre, 1, 1)
                ) - (pltpu.roll(centre, depth - 2, 1) - pltpu.roll(centre, 2, 1))
                grads.append((along_x, along_y, along_z))
            inner = grads[0][0] * grads[0][0] + grads[1][1] * grads[1][1] + grads[2][2] * grads[2][2]
            inner = inner + 2.0 * (
                grads[0][1] * grads[1][0] + grads[0][2] * grads[2][0] + grads[1][2] * grads[2][1]
            )
            scaled[x] = (-50.0 / 144.0) * inner
            return carry

        for x in range(width + 1):
            criterion(x, 0)

        for copy in copies:
            copy.wait()
        brick_x, brick_y = (ix * width) // BRICK, (iy * height) // BRICK
        chosen = index[brick_x, brick_y]
        level = jnp.float32(0.0)
        for number in range(levels.shape[0]):
            level = jnp.where(chosen == number, levels[number], level)
        lane = lax.broadcasted_iota(jnp.int32, (height, depth), 1) // BRICK
        seen = jnp.zeros((height, depth), jnp.int32)
        for number in range(depth // BRICK):
            seen = jnp.where(lane == number, visible[brick_x, brick_y, number], seen)
        shown = seen == 1

        def edges(x, carry):
            inside = scaled[x, 0:height, :]
            here = inside - level
            square = here * here + 0.25
            q_out[x] = jnp.where(shown, inside, 0.0)
            theres = (
                scaled[x + 1, 0:height, :] - level,
                scaled[x, 1 : 1 + height, :] - level,
                pltpu.roll(here, depth - 1, 1),
            )
            for direction, there in enumerate(theres):
                weight = jnp.maximum(-here * there, 0.0) / (square + there * there)
                cross_out[direction, x] = jnp.where(shown, weight, 0.0)
            return carry

        for x in range(width):
            edges(x, 0)
        last = [
            pltpu.make_async_copy(q_out, q_hbm, out_sem.at[1]),
            pltpu.make_async_copy(cross_out, cross_hbm, out_sem.at[2]),
        ]
        for copy in last:
            copy.start()
        new_copy.wait()
        for copy in last:
            copy.wait()

    return kernel


def solution(mesh):
    sizes = (mesh.shape["gx"], mesh.shape["gy"])

    def per_device(populations, solid, visible, omega, iso_levels, iso_index):
        _, width, height, depth = populations.shape
        rows = PAD + height + 8
        f32 = jnp.float32
        messages = [
            pltpu.VMEM((message_rows(unit, width, height), depth), f32) for unit in UNITS
        ]
        far = pl.BlockSpec(memory_space=pltpu.HBM)
        near = pl.BlockSpec(memory_space=pltpu.VMEM)
        moved, total = pl.pallas_call(
            kernel_of(sizes, width, height, depth),
            out_shape=(
                jax.ShapeDtypeStruct((19, width + 2, rows, depth), f32),
                jax.ShapeDtypeStruct((4, width + 5, rows, depth), f32),
            ),
            in_specs=[far, far, near],
            out_specs=(near, near),
            scratch_shapes=[
                pltpu.VMEM(populations.shape, f32),
                pltpu.VMEM(solid.shape, jnp.int32),
            ]
            + messages
            + messages
            + [
                pltpu.SemaphoreType.DMA((1 + CHUNKS,)),
                pltpu.SemaphoreType.DMA((len(UNITS),)),
                pltpu.SemaphoreType.DMA((len(UNITS),)),
            ],
            compiler_params=pltpu.CompilerParams(
                collective_id=0, has_side_effects=True, vmem_limit_bytes=24 * 1024 * 1024
            ),
        )(
            pltpu.with_memory_space_constraint(populations, pltpu.HBM),
            pltpu.with_memory_space_constraint(solid, pltpu.HBM),
            jnp.broadcast_to(omega, (8, depth)),
        )
        return pl.pallas_call(
            finish_of(width, height, depth),
            out_shape=(
                jax.ShapeDtypeStruct(populations.shape, f32),
                jax.ShapeDtypeStruct((width, height, depth), f32),
                jax.ShapeDtypeStruct((3, width, height, depth), f32),
            ),
            in_specs=[near, near, far, far, far],
            out_specs=(far, far, far),
            scratch_shapes=[
                pltpu.SMEM(visible.shape, jnp.int32),
                pltpu.SMEM(iso_levels.shape, f32),
                pltpu.SMEM(iso_index.shape, jnp.int32),
                pltpu.VMEM((3, width + 5, rows + 8, depth), f32),
                pltpu.VMEM((width + 1, height + 8, depth), f32),
                pltpu.VMEM((width, height, depth), f32),
                pltpu.VMEM((3, width, height, depth), f32),
                pltpu.SemaphoreType.DMA((3,)),
                pltpu.SemaphoreType.DMA((3,)),
            ],
            compiler_params=pltpu.CompilerParams(vmem_limit_bytes=24 * 1024 * 1024),
        )(moved, total, visible, iso_levels, iso_index)

    in_specs = (P(None, "gx", "gy", None), P("gx", "gy", None), P(), P(), P(), P())
    out_specs = (P(None, "gx", "gy", None), P("gx", "gy", None), P(None, "gx", "gy", None))
    return jax.shard_map(
        per_device, mesh=mesh, in_specs=in_specs, out_specs=out_specs, check_vma=False
    )
```

```python
import jax
import jax.numpy as jnp
from jax import lax
from jax.experimental import pallas as pl
from jax.experimental.pallas import tpu as pltpu
from jax.sharding import PartitionSpec as P

BRICK = 16
LATTICE = [
    (0, 0, 0),
    (1, 0, 0),
    (-1, 0, 0),
    (0, 1, 0),
    (0, -1, 0),
    (0, 0, 1),
    (0, 0, -1),
    (1, 1, 0),
    (-1, -1, 0),
    (1, -1, 0),
    (-1, 1, 0),
    (1, 0, 1),
    (-1, 0, -1),
    (1, 0, -1),
    (-1, 0, 1),
    (0, 1, 1),
    (0, -1, -1),
    (0, 1, -1),
    (0, -1, 1),
]
OPPOSITE = [0, 2, 1, 4, 3, 6, 5, 8, 7, 10, 9, 12, 11, 14, 13, 16, 15, 18, 17]
DIRECTIONS = [(-1, 0), (1, 0), (0, -1), (0, 1), (-1, -1), (-1, 1), (1, -1), (1, 1)]
MESH = pl.DeviceIdType.MESH
CHUNKS = 4
PAD = 8


def needed_halo(width, height):
    cells = set()
    for x in range(width + 1):
        for y in range(height + 1):
            if x == width and y == height:
                continue
            for step in range(-2, 3):
                cells.add((x + step, y))
                cells.add((x, y + step))
    return {(x, y) for x, y in cells if not (0 <= x < width and 0 <= y < height)}


def message_plan(direction, width, height):
    sx, sy = direction
    halo = needed_halo(width, height)
    pops = [
        k
        for k, c in enumerate(LATTICE)
        if (sx == 0 or c[0] == sx) and (sy == 0 or c[1] == sy)
    ]
    layers, cells = [], []
    if sx and not sy:
        layers = [0, 1, 2] if sx < 0 else [width - 2, width - 1]
    if sy and not sx:
        layers = [0, 1, 2] if sy < 0 else [height - 2, height - 1]
    for x in range(-1, width + 1):
        for y in range(-1, height + 1):
            if (x - sx * width, y - sy * height) not in halo:
                continue
            if sx and sy:
                cells.append((x, y))
            elif sx and 0 <= x < width and not 0 <= y < height:
                cells.append((x, y))
            elif sy and 0 <= y < height and not 0 <= x < width:
                cells.append((x, y))
    return pops, layers, cells


def touches(direction, layer, width, height):
    sx, sy = direction
    return layer == (0 if sx + sy < 0 else (width if sx else height) - 1)


UNITS = (
    [(number, True, False) for number in (2, 3, 0, 1)]
    + [(number, False, True) for number in (2, 3)]
    + [(number, True, True) for number in (4, 5, 6, 7)]
    + [(number, False, True) for number in (0, 1)]
)


def message_rows(unit, width, height):
    number, with_pops, with_sums = unit
    direction = DIRECTIONS[number]
    pops, layers, cells = message_plan(direction, width, height)
    pops = pops if with_pops else []
    layers, cells = (layers, cells) if with_sums else ([], [])
    line = 1 if direction[0] and direction[1] else (height if direction[0] else width)
    rows = len(pops) * line + 4 * len(cells)
    for layer in layers:
        rows += 4 * line if touches(direction, layer, width, height) else 3 * line + 2
    for x, y in cells:
        rows -= 0 if 0 <= x < width and 0 <= y < height else 1
    return -(-rows // 8) * 8


def sums(read):
    n11, n12, n13, n14 = read(11), read(12), read(13), read(14)
    n15, n16, n17, n18 = read(15), read(16), read(17), read(18)
    east = (read(1) + n11) + n13
    west = (read(2) + n12) + n14
    north = (read(3) + n15) + n17
    south = (read(4) + n16) + n18
    n5, n6, n7, n8, n9, n10 = read(5), read(6), read(7), read(8), read(9), read(10)
    density = ((read(0) + n5) + n6) + (east + west) + (north + south) + ((n7 + n8) + (n9 + n10))
    momentum_x = (east - west) + ((n7 - n8) + (n9 - n10))
    momentum_y = (north - south) + ((n7 - n8) - (n9 - n10))
    momentum_z = (n5 - n6) + ((n11 - n12) - (n13 - n14)) + ((n15 - n16) - (n17 - n18))
    return density, momentum_x, momentum_y, momentum_z


def kernel_of(sizes, width, height, depth):
    size_x, size_y = sizes
    plans = [message_plan(d, width, height) for d in DIRECTIONS]

    def kernel(pop_hbm, solid_hbm, omega_rows, moved, total, pop, solid, *rest):
        count = len(UNITS)
        sends, recvs = rest[:count], rest[count : 2 * count]
        in_sem, send_sem, recv_sem = rest[2 * count :]
        ix, iy = lax.axis_index("gx"), lax.axis_index("gy")
        layers = width // CHUNKS
        copies = [
            pltpu.make_async_copy(src, dst, in_sem.at[i])
            for i, (src, dst) in enumerate(
                [(solid_hbm, solid)]
                + [
                    (pop_hbm.at[:, pl.ds(c * layers, layers)], pop.at[:, pl.ds(c * layers, layers)])
                    for c in range(CHUNKS)
                ]
            )
        ]
        targets = [
            (lax.rem(ix + sx + size_x, size_x), lax.rem(iy + sy + size_y, size_y))
            for sx, sy in DIRECTIONS
        ]
        barrier = pltpu.get_barrier_semaphore()
        for target in targets:
            pl.semaphore_signal(barrier, inc=1, device_id=target, device_id_type=MESH)
        for copy in copies:
            copy.start()

        rows = moved.shape[2]
        blank = jnp.zeros((rows, depth), jnp.float32)

        def clear(x, carry):
            for k in range(19):
                moved[k, x] = blank
            return carry

        lax.fori_loop(0, width + 2, clear, 0)
        for x in (0, width + 3, width + 4):
            for c in range(4):
                total[c, x] = blank
        for copy in copies[:1]:
            copy.wait()

        rate = omega_rows[0:1, :]
        keep = 1.0 - rate

        def collide(x, carry):
            p = [pop[k, x] for k in range(19)]
            wall = solid[x] == 1
            density, mx, my, mz = sums(lambda k: p[k])
            inverse = 1.0 / density
            velocity = (mx * inverse, my * inverse, mz * inverse)
            base = 1.0 - 1.5 * (
                velocity[0] * velocity[0] + velocity[1] * velocity[1] + velocity[2] * velocity[2]
            )
            scale = rate * density
            heavy, light = scale * (1.0 / 18.0), scale * (1.0 / 36.0)

            def put(k, value):
                cx, cy, cz = LATTICE[k]
                value = jnp.where(wall, p[OPPOSITE[k]], value)
                if cz:
                    value = pltpu.roll(value, cz % depth, 1)
                moved[k, x + (1 + cx), PAD + cy : PAD + cy + height, :] = value

            put(0, keep * p[0] + (scale * (1.0 / 3.0)) * base)
            for k in range(1, 19, 2):
                projection = None
                for direction in range(3):
                    component = LATTICE[k][direction]
                    if component:
                        term = velocity[direction]
                        if projection is None:
                            projection = term if component == 1 else -term
                        else:
                            projection = projection + term if component == 1 else projection - term
                weight = heavy if k < 7 else light
                even = base + 4.5 * (projection * projection)
                odd = 3.0 * projection
                put(k, keep * p[k] + weight * (even + odd))
                put(k + 1, keep * p[k + 1] + weight * (even - odd))
            return carry

        for c in range(CHUNKS):
            copies[1 + c].wait()
            for x in range(c * layers, (c + 1) * layers):
                collide(x, 0)

        def pieces(unit):
            number, with_pops, with_sums = UNITS[unit]
            sx, sy = DIRECTIONS[number]
            pops, layers, cells = plans[number]
            pops = pops if with_pops else []
            layers, cells = (layers, cells) if with_sums else ([], [])
            at, found = 0, []
            from_x = {-1: 0, 0: None, 1: width - 1}[sx]
            from_y = {-1: 0, 0: None, 1: height - 1}[sy]
            for k in pops:
                cx, cy, _ = LATTICE[k]
                if sy == 0:
                    y = slice(PAD + cy, PAD + cy + height)
                    here, there = (k, from_x + cx + 1, y), (k, from_x + cx + 1 - sx * width, y)
                    length = height
                elif sx == 0:
                    x = slice(1 + cx, 1 + cx + width)
                    here = (k, x, PAD + from_y + cy)
                    there = (k, x, PAD + from_y + cy - sy * height)
                    length = width
                else:
                    x, y = from_x + cx + 1, PAD + from_y + cy
                    here = (k, x, slice(y, y + 1))
                    there = (k, x - sx * width, slice(y - sy * height, y - sy * height + 1))
                    length = 1
                found.append(("pop", at, length, here, there))
                at += length
            for layer in layers:
                whole = touches(DIRECTIONS[number], layer, width, height)
                for c in range(0 if whole else 1, 4):
                    if sy == 0:
                        y = slice(PAD, PAD + height)
                        here, there = (c, layer + 2, y), (c, layer + 2 - sx * width, y)
                        length = height
                    else:
                        here = (c, slice(2, 2 + width), PAD + layer)
                        there = (c, slice(2, 2 + width), PAD + layer - sy * height)
                        length = width
                    found.append(("sum" if whole else "flow", at, length, here, there))
                    at += length
                for edge in () if whole else (0, (height if sy == 0 else width) - 1):
                    x, y = (layer, edge) if sy == 0 else (edge, layer)
                    row = slice(PAD + y, PAD + y + 1)
                    to = PAD + y - sy * height
                    there = (0, x + 2 - sx * width, slice(to, to + 1))
                    found.append(("sum", at, 1, (0, x + 2, row), there))
                    at += 1
            for x, y in cells:
                for c in range(4):
                    if (c == 1 and not 0 <= x < width) or (c == 2 and not 0 <= y < height):
                        continue
                    here = (c, x + 2, slice(PAD + y, PAD + y + 1))
                    to = PAD + y - sy * height
                    there = (c, x + 2 - sx * width, slice(to, to + 1))
                    kind = "sum"
                    if c == 0 and not 0 <= x < width:
                        kind = ("also", 1, x < 0)
                    if c == 0 and not 0 <= y < height:
                        kind = ("also", 2, y < 0)
                    found.append((kind, at, 1, here, there))
                    at += 1
            return found

        remote = {}

        def inner(length):
            place = lax.broadcasted_iota(jnp.int32, (length, depth), 0)
            return jnp.logical_and(place > 0, place < length - 1)

        def send(unit):
            inverses = {}
            for kind, at, length, here, _ in pieces(unit):
                value = moved[here] if kind == "pop" else total[here]
                if kind == "flow":
                    key = str(here[1:])
                    if key not in inverses:
                        density = total[(0,) + here[1:]]
                        inverses[key] = jnp.where(inner(length), 1.0 / density, 1.0)
                    value = value * inverses[key]
                sends[unit][at : at + length, :] = value
            copy = pltpu.make_async_remote_copy(
                src_ref=sends[unit],
                dst_ref=recvs[unit],
                send_sem=send_sem.at[unit],
                recv_sem=recv_sem.at[unit],
                device_id=targets[UNITS[unit][0]],
                device_id_type=MESH,
            )
            copy.start()
            remote[unit] = copy

        pl.semaphore_wait(barrier, 8)
        for unit in range(4):
            send(unit)

        def own_part(x, carry):
            for c, value in enumerate(sums(lambda k: moved[k, x, 4 : rows - 4, :])):
                total[c, x + 1, 4 : rows - 4, :] = value
            return carry

        for x in range(width + 2):
            own_part(x, 0)

        for unit in range(4, count):
            send(unit)

        for unit in (2, 3, 0, 1, 6, 7, 8, 9, 10, 11, 4, 5):
            remote[unit].wait_recv()
            groups = {}
            for kind, at, length, _, there in pieces(unit):
                value = recvs[unit][at : at + length, :]
                if kind != "pop":
                    total[there] = total[there] + value
                    if kind == "flow" and there[0] == 1:
                        density = (0,) + there[1:]
                        total[density] = total[density] + jnp.where(inner(length), 1.0, 0.0)
                    if kind[0] == "also":
                        c = (kind[1],) + there[1:]
                        total[c] = total[c] + (-value if kind[2] else value)
                    continue
                moved[there] = value
                k, x, y = there
                x = slice(x.start + 1, x.stop + 1) if isinstance(x, slice) else x + 1
                groups.setdefault(LATTICE[k][:2], []).append((LATTICE[k][2], value, x, y))
            for (cx, cy), members in groups.items():
                _, value, x, y = members[0]
                along_z = None
                for cz, other, _, _ in members[1:]:
                    value = value + other
                if len(members) == 3:
                    up = [other for cz, other, _, _ in members if cz == 1][0]
                    down = [other for cz, other, _, _ in members if cz == -1][0]
                    along_z = up - down
                total[0, x, y] = total[0, x, y] + value
                for c, sign in ((1, cx), (2, cy)):
                    if sign:
                        total[c, x, y] = total[c, x, y] + (value if sign == 1 else -value)
                if along_z is not None:
                    total[3, x, y] = total[3, x, y] + along_z

        for copy in remote.values():
            copy.wait_send()

    return kernel


def finish_of(width, height, depth):
    def kernel(moved, total, visible_hbm, levels_hbm, index_hbm, new_hbm, q_hbm, cross_hbm,
               visible, levels, index, flow, scaled, q_out, cross_out, in_sem, out_sem):
        new_copy = pltpu.make_async_copy(
            moved.at[:, 1 : 1 + width, PAD : PAD + height, :], new_hbm, out_sem.at[0]
        )
        new_copy.start()
        copies = [
            pltpu.make_async_copy(src, dst, in_sem.at[i])
            for i, (src, dst) in enumerate(
                [(visible_hbm, visible), (levels_hbm, levels), (index_hbm, index)]
            )
        ]
        for copy in copies:
            copy.start()
        ix, iy = lax.axis_index("gx"), lax.axis_index("gy")
        rows = total.shape[2]

        def divide(x, carry):
            inverse = 1.0 / total[0, x, 4 : rows - 4, :]
            for a in range(3):
                flow[a, x, 4 : rows - 4, :] = total[a + 1, x, 4 : rows - 4, :] * inverse
            return carry

        for x in range(width + 5):
            divide(x, 0)

        tall = height + 8

        def criterion(x, carry):
            grads = []
            for a in range(3):
                def at(dx, dy):
                    return flow[a, x + 2 + dx, PAD + dy : PAD + dy + tall, :]

                centre = at(0, 0)
                along_x = 8.0 * (at(1, 0) - at(-1, 0)) - (at(2, 0) - at(-2, 0))
                along_y = 8.0 * (at(0, 1) - at(0, -1)) - (at(0, 2) - at(0, -2))
                along_z = 8.0 * (
                    pltpu.roll(centre, depth - 1, 1) - pltpu.roll(centre, 1, 1)
                ) - (pltpu.roll(centre, depth - 2, 1) - pltpu.roll(centre, 2, 1))
                grads.append((along_x, along_y, along_z))
            inner = grads[0][0] * grads[0][0] + grads[1][1] * grads[1][1] + grads[2][2] * grads[2][2]
            inner = inner + 2.0 * (
                grads[0][1] * grads[1][0] + grads[0][2] * grads[2][0] + grads[1][2] * grads[2][1]
            )
            scaled[x] = (-50.0 / 144.0) * inner
            return carry

        for x in range(width + 1):
            criterion(x, 0)

        for copy in copies:
            copy.wait()
        brick_x, brick_y = (ix * width) // BRICK, (iy * height) // BRICK
        chosen = index[brick_x, brick_y]
        level = jnp.float32(0.0)
        for number in range(levels.shape[0]):
            level = jnp.where(chosen == number, levels[number], level)
        lane = lax.broadcasted_iota(jnp.int32, (height, depth), 1) // BRICK
        seen = jnp.zeros((height, depth), jnp.int32)
        for number in range(depth // BRICK):
            seen = jnp.where(lane == number, visible[brick_x, brick_y, number], seen)
        shown = seen == 1

        def edges(x, carry):
            inside = scaled[x, 0:height, :]
            here = inside - level
            square = here * here + 0.25
            q_out[x] = jnp.where(shown, inside, 0.0)
            theres = (
                scaled[x + 1, 0:height, :] - level,
                scaled[x, 1 : 1 + height, :] - level,
                pltpu.roll(here, depth - 1, 1),
            )
            for direction, there in enumerate(theres):
                weight = jnp.maximum(-here * there, 0.0) / (square + there * there)
                cross_out[direction, x] = jnp.where(shown, weight, 0.0)
            return carry

        for x in range(width):
            edges(x, 0)
        last = [
            pltpu.make_async_copy(q_out, q_hbm, out_sem.at[1]),
            pltpu.make_async_copy(cross_out, cross_hbm, out_sem.at[2]),
        ]
        for copy in last:
            copy.start()
        new_copy.wait()
        for copy in last:
            copy.wait()

    return kernel


def solution(mesh):
    sizes = (mesh.shape["gx"], mesh.shape["gy"])

    def per_device(populations, solid, visible, omega, iso_levels, iso_index):
        _, width, height, depth = populations.shape
        rows = PAD + height + 8
        f32 = jnp.float32
        messages = [
            pltpu.VMEM((message_rows(unit, width, height), depth), f32) for unit in UNITS
        ]
        far = pl.BlockSpec(memory_space=pltpu.HBM)
        near = pl.BlockSpec(memory_space=pltpu.VMEM)
        moved, total = pl.pallas_call(
            kernel_of(sizes, width, height, depth),
            out_shape=(
                jax.ShapeDtypeStruct((19, width + 2, rows, depth), f32),
                jax.ShapeDtypeStruct((4, width + 5, rows, depth), f32),
            ),
            in_specs=[far, far, near],
            out_specs=(near, near),
            scratch_shapes=[
                pltpu.VMEM(populations.shape, f32),
                pltpu.VMEM(solid.shape, jnp.int32),
            ]
            + messages
            + messages
            + [
                pltpu.SemaphoreType.DMA((1 + CHUNKS,)),
                pltpu.SemaphoreType.DMA((len(UNITS),)),
                pltpu.SemaphoreType.DMA((len(UNITS),)),
            ],
            compiler_params=pltpu.CompilerParams(
                collective_id=0, has_side_effects=True, vmem_limit_bytes=24 * 1024 * 1024
            ),
        )(
            pltpu.with_memory_space_constraint(populations, pltpu.HBM),
            pltpu.with_memory_space_constraint(solid, pltpu.HBM),
            jnp.broadcast_to(omega, (8, depth)),
        )
        return pl.pallas_call(
            finish_of(width, height, depth),
            out_shape=(
                jax.ShapeDtypeStruct(populations.shape, f32),
                jax.ShapeDtypeStruct((width, height, depth), f32),
                jax.ShapeDtypeStruct((3, width, height, depth), f32),
            ),
            in_specs=[near, near, far, far, far],
            out_specs=(far, far, far),
            scratch_shapes=[
                pltpu.SMEM(visible.shape, jnp.int32),
                pltpu.SMEM(iso_levels.shape, f32),
                pltpu.SMEM(iso_index.shape, jnp.int32),
                pltpu.VMEM((3, width + 5, rows + 8, depth), f32),
                pltpu.VMEM((width + 1, height + 8, depth), f32),
                pltpu.VMEM((width, height, depth), f32),
                pltpu.VMEM((3, width, height, depth), f32),
                pltpu.SemaphoreType.DMA((3,)),
                pltpu.SemaphoreType.DMA((3,)),
            ],
            compiler_params=pltpu.CompilerParams(vmem_limit_bytes=24 * 1024 * 1024),
        )(moved, total, visible, iso_levels, iso_index)

    in_specs = (P(None, "gx", "gy", None), P("gx", "gy", None), P(), P(), P(), P())
    out_specs = (P(None, "gx", "gy", None), P("gx", "gy", None), P(None, "gx", "gy", None))
    return jax.shard_map(
        per_device, mesh=mesh, in_specs=in_specs, out_specs=out_specs, check_vma=False
    )
```
